256 devices in a mesh: gx: 8 (over y, z_lo), gy: 4 (over z_hi), gz: 8 (over x, core).
Axes of the slice: x: 4, y: 4, z: 8 (z_hi: 4, z_lo: 2; z = z_hi * 2 + z_lo), core: 2. Of those that a mesh axis runs over, the one named last changes fastest.
Arguments:
- features: bfloat16 [64, 4, 8, 64, 128], P('gx', 'gy', 'gz'), may hold values from -6 to 6
- positions: bfloat16 [64, 4, 8, 3, 128], P('gx', 'gy', 'gz'), may hold values from 0 to 1
- counts: int32 [64, 4, 8], P('gx', 'gy', 'gz'), may hold values from 1 to 128, as said below
- old_cuts: int32 [9], replicated, may hold values from 0 to 32, as said below
- new_cuts: int32 [9], replicated, may hold values from 0 to 32, as said below
- radial_rates: float32 [2, 2], replicated, may hold values from 0.3 to 3
- conv_weight: bfloat16 [2, 64, 2, 64], replicated, may hold values from -0.5 to 0.5
- up_weight: bfloat16 [2, 256, 64], replicated, may hold values from -0.75 to 0.75
- up_bias: float32 [2, 256], replicated, may hold values from -3 to 3
- down_weight: bfloat16 [2, 64, 256], replicated, may hold values from -0.375 to 0.375
- down_bias: float32 [2, 64], replicated, may hold values from -2 to 2
Outputs:
- moved: bfloat16 [64, 4, 8, 64, 128], P('gx', 'gy', 'gz')
The draws below stay inside these ranges and needn't reach their ends.
Inputs may be any that keep to these rules, and one draw needn't show every extreme that they name: `counts`: some bin of the first x layer holds exactly 128 particles. `old_cuts`: rising from 0 to 32; index k of gx holds the x layers from old_cuts[k] to old_cuts[k+1] - 1, from 2 to 8 of them; with three or more indices along gx one holds exactly 8. `new_cuts`: same form as old_cuts, and each cut differs from the one of old_cuts by -1, 0 or 1.
All inputs are finite; a program needn't handle non-finite values.
Results may differ from the reference program's by a relative error of at most 0.0058.
Values may be sent and summed in bfloat16 or wider, within the bound.
A program may use at most 128 MiB of HBM per device.

```python
import math
import jax
import jax.numpy as jnp
from jax import lax

F = 64
HID = 256
RADIAL = 2
PSLOT = 128
LAYERS = 2
XL = 4
LCAP = 8
SLOTS = 64
NY = 4
NZ = 8
N_GX = 8


def cut_pair(key):
    base_key = jax.random.fold_in(key, 7)
    key_order, key_pairs, key_moves = jax.random.split(base_key, 3)
    shuffled = jax.random.permutation(key_order, N_GX)
    layer_counts = jnp.full((N_GX,), XL, jnp.int32)
    extra_layers = min(XL, (XL - 2) * (N_GX - 1))
    layer_counts = layer_counts.at[shuffled[0]].add(extra_layers)
    remain = extra_layers
    next_place = 1
    for rank_place in range(1, N_GX):
        taken_layers = min(XL - 2, remain)
        if taken_layers > 0:
            layer_counts = layer_counts.at[shuffled[rank_place]].add(-taken_layers)
            next_place = rank_place + 1
        remain = remain - taken_layers
    pair_count = (N_GX - next_place) // 2
    if pair_count > 0:
        swings = jax.random.randint(key_pairs, (pair_count,), -1, 2).astype(jnp.int32)
        layer_counts = layer_counts.at[shuffled[next_place:next_place + pair_count]].add(swings)
        layer_counts = layer_counts.at[shuffled[next_place + pair_count:next_place + 2 * pair_count]].add(-swings)
    zero_cut = jnp.zeros((1,), jnp.int32)
    old_drawn = jnp.concatenate([zero_cut, jnp.cumsum(layer_counts).astype(jnp.int32)])
    inner_low = layer_counts[:-1]
    inner_high = layer_counts[1:]
    signs = (2 * jax.random.randint(key_moves, (N_GX - 1,), 0, 2) - 1).astype(jnp.int32)
    down_ok = (inner_low >= 3) & (inner_high <= LCAP - 1)
    up_ok = (inner_high >= 3) & (inner_low <= LCAP - 1)
    first_ok = jnp.where(signs < 0, down_ok, up_ok)
    second_ok = jnp.where(signs < 0, up_ok, down_ok)
    cut_moves = jnp.where(first_ok, signs, jnp.where(second_ok, -signs, 0)).astype(jnp.int32)
    odd_cut = jnp.arange(1, N_GX, dtype=jnp.int32) % 2 == 1
    cut_moves = jnp.where(odd_cut, cut_moves, 0).astype(jnp.int32)
    new_drawn = old_drawn + jnp.concatenate([zero_cut, cut_moves, zero_cut])
    return (old_drawn, new_drawn)


def draw_old_cuts(key, part):
    return cut_pair(key)[0]


def draw_new_cuts(key, part):
    return cut_pair(key)[1]


def draw_counts(key, part):
    base_key = jax.random.fold_in(key, 11)
    key_counts, key_y, key_z = jax.random.split(base_key, 3)
    drawn_counts = jax.random.randint(key_counts, (SLOTS, NY, NZ), 1, PSLOT + 1).astype(jnp.int32)
    chosen_y = jax.random.randint(key_y, (), 0, NY)
    chosen_z = jax.random.randint(key_z, (), 0, NZ)
    return drawn_counts.at[0, chosen_y, chosen_z].set(PSLOT)


def levels(rng, extent, cuts, least, high):
    gain = 1.0
    for position, parts in cuts:
        steps = jax.random.uniform(jax.random.fold_in(jax.random.fold_in(rng, 6), position), (parts,), jnp.float32, least / len(cuts), high / len(cuts))
        gain = gain * jnp.repeat(jnp.exp(steps), extent[position] // parts).reshape((-1,) + (1,) * (len(extent) - 1 - position))
    return gain


def bell_draw(rng, dims, width, bound, shards=(), held_as=jnp.bfloat16):
    loudness = levels(rng, dims, shards, -0.22, 0.18) if shards else 1.0
    entries = jax.random.normal(rng, dims, jnp.float32) * width * loudness
    return jnp.minimum(jnp.maximum(entries, -bound), bound).astype(held_as)


def setup_inputs(seed: int = 0) -> dict:
    keys = jax.random.split(jax.random.key(seed), 12)
    features = bell_draw(keys[0], (SLOTS, NY, NZ, F, PSLOT), 1.0, 6.0, ((0, 8), (1, 4), (2, 8)))
    positions = jnp.clip(1.0 * jax.random.uniform(keys[1], (SLOTS, NY, NZ, 3, PSLOT), jnp.float32) ** levels(keys[1], (SLOTS, NY, NZ, 3, PSLOT), ((0, 8), (1, 4), (2, 8)), -0.2, 0.2), 0.0, 1.0).astype(jnp.bfloat16)
    counts = draw_counts(jax.random.fold_in(keys[11], 71), 0)
    old_cuts = draw_old_cuts(jax.random.fold_in(keys[11], 71), 0)
    new_cuts = draw_new_cuts(jax.random.fold_in(keys[11], 71), 0)
    radial_rates = jnp.clip(jnp.exp(jax.random.uniform(keys[5], (LAYERS, RADIAL), jnp.float32, math.log(0.3), math.log(3.0))), 0.3, 3.0)
    conv_weight = bell_draw(keys[6], (LAYERS, F, RADIAL, F), (RADIAL * F) ** -0.5, 0.5)
    up_weight = bell_draw(keys[7], (LAYERS, HID, F), F ** -0.5, 0.75)
    up_bias = bell_draw(keys[8], (LAYERS, HID), 0.5, 3.0, (), jnp.float32)
    down_weight = bell_draw(keys[9], (LAYERS, F, HID), HID ** -0.5, 0.375)
    down_bias = bell_draw(keys[10], (LAYERS, F), 0.3, 2.0, (), jnp.float32)
    return dict(features=features, positions=positions, counts=counts, old_cuts=old_cuts, new_cuts=new_cuts, radial_rates=radial_rates, conv_weight=conv_weight, up_weight=up_weight, up_bias=up_bias, down_weight=down_weight, down_bias=down_bias)


EPSILON = 1e-05

def convolve(features, positions, counts, live_rows, decay_rates, conv_weight, up_weight, up_bias, down_weight, down_bias):
    deep_rows = features.shape[0] - 2
    rows_y = features.shape[1] - 2
    rows_z = features.shape[2] - 2
    feature_count = features.shape[3]
    slot_count = features.shape[4]
    bin_count = deep_rows * rows_y * rows_z
    slot_index = jnp.arange(slot_count, dtype=jnp.int32)
    present = (slot_index < counts[..., None]).astype(jnp.float32)
    centre_positions = positions[1:-1, 1:-1, 1:-1].astype(jnp.float32).reshape(bin_count, 3, slot_count)
    summed = jnp.zeros((bin_count, feature_count, decay_rates.shape[0], slot_count), jnp.float32)
    for step_x in (-1, 0, 1):
        for step_y in (-1, 0, 1):
            for step_z in (-1, 0, 1):
                near_features = features[1 + step_x:1 + step_x + deep_rows, 1 + step_y:1 + step_y + rows_y, 1 + step_z:1 + step_z + rows_z].reshape(bin_count, feature_count, slot_count)
                near_positions = positions[1 + step_x:1 + step_x + deep_rows, 1 + step_y:1 + step_y + rows_y, 1 + step_z:1 + step_z + rows_z].astype(jnp.float32).reshape(bin_count, 3, slot_count)
                near_valid = present[1 + step_x:1 + step_x + deep_rows, 1 + step_y:1 + step_y + rows_y, 1 + step_z:1 + step_z + rows_z].reshape(bin_count, slot_count)
                offset = jnp.array([step_x, step_y, step_z], jnp.float32)
                spread = offset[None, :, None, None] + centre_positions[:, :, :, None] - near_positions[:, :, None, :]
                distance = spread[:, 0] * spread[:, 0] + spread[:, 1] * spread[:, 1] + spread[:, 2] * spread[:, 2]
                kernel = (jnp.exp(-decay_rates[None, :, None, None] * distance[:, None]) * near_valid[:, None, None, :]).astype(jnp.bfloat16)
                summed = summed + jnp.einsum('bfj,bmij->bfmi', near_features.astype(jnp.float32), kernel.astype(jnp.float32))
    gathered = summed.astype(jnp.bfloat16)
    mixed_rows = jnp.einsum('omf,bfmi->boi', conv_weight.astype(jnp.float32), gathered.astype(jnp.float32))
    centred = mixed_rows - lax.optimization_barrier(jnp.mean(mixed_rows, axis=1, keepdims=True))
    normed = (centred * lax.rsqrt(lax.optimization_barrier(jnp.mean(centred * centred, axis=1, keepdims=True)) + EPSILON)).astype(jnp.bfloat16)
    hidden = jax.nn.silu(jnp.einsum('ho,boi->bhi', up_weight.astype(jnp.float32), normed.astype(jnp.float32)) + up_bias[None, :, None]).astype(jnp.bfloat16)
    update = jnp.einsum('oh,bhi->boi', down_weight.astype(jnp.float32), hidden.astype(jnp.float32)) + down_bias[None, :, None]
    centre_features = features[1:-1, 1:-1, 1:-1].reshape(bin_count, feature_count, slot_count).astype(jnp.float32)
    keep_mask = (present[1:-1, 1:-1, 1:-1] * live_rows[:, None, None, None]).reshape(bin_count, 1, slot_count)
    result = ((centre_features + update) * keep_mask).astype(jnp.bfloat16)
    return result.reshape(deep_rows, rows_y, rows_z, feature_count, slot_count)

def to_global(array_in, cuts):
    layer_total = XL * N_GX
    layer_index = jnp.arange(layer_total, dtype=jnp.int32)
    owner_rank = lax.optimization_barrier(jnp.sum((cuts[1:N_GX][None, :] <= layer_index[:, None]).astype(jnp.int32), axis=1)).astype(jnp.int32)
    source = (owner_rank * LCAP + layer_index - cuts[owner_rank]).astype(jnp.int32)
    return jnp.take(array_in, source, axis=0)

def to_slots(array_in, cuts):
    slot_place = jnp.arange(N_GX * LCAP, dtype=jnp.int32)
    owner_rank = slot_place // LCAP
    local_slot = slot_place % LCAP
    layer_index = (cuts[owner_rank] + local_slot).astype(jnp.int32)
    alive_slot = local_slot < cuts[owner_rank + 1] - cuts[owner_rank]
    picked = jnp.take(array_in, jnp.clip(layer_index, 0, XL * N_GX - 1), axis=0)
    return jnp.where(alive_slot[:, None, None, None, None], picked, jnp.zeros_like(picked))

def run_layer(features, positions, counts, decay_rates, conv_weight, up_weight, up_bias, down_weight, down_bias):
    layer_total = features.shape[0]
    padding = ((1, 1), (1, 1), (1, 1), (0, 0), (0, 0))
    padded_features = jnp.pad(features, padding)
    padded_positions = jnp.pad(positions, padding)
    padded_counts = jnp.pad(counts, 1)
    live_rows = jnp.ones((1,), jnp.float32)

    def one_layer(start_row):
        return convolve(lax.dynamic_slice_in_dim(padded_features, start_row, 3, 0), lax.dynamic_slice_in_dim(padded_positions, start_row, 3, 0), lax.dynamic_slice_in_dim(padded_counts, start_row, 3, 0), live_rows, decay_rates, conv_weight, up_weight, up_bias, down_weight, down_bias)[0]
    return lax.map(one_layer, jnp.arange(layer_total, dtype=jnp.int32))

def reference(features, positions, counts, old_cuts, new_cuts, radial_rates, conv_weight, up_weight, up_bias, down_weight, down_bias):
    grid_features = to_global(features, old_cuts)
    grid_positions = to_global(positions, old_cuts)
    grid_counts = to_global(counts, old_cuts)
    first_out = run_layer(grid_features, grid_positions, grid_counts, radial_rates[0], conv_weight[0], up_weight[0], up_bias[0], down_weight[0], down_bias[0])
    second_out = run_layer(first_out, grid_positions, grid_counts, radial_rates[1], conv_weight[1], up_weight[1], up_bias[1], down_weight[1], down_bias[1])
    return to_slots(second_out, new_cuts)
```

```python
import jax
import jax.numpy as jnp
from jax import lax
from jax.experimental import pallas as pl
from jax.experimental.pallas import tpu as pltpu
from jax.sharding import PartitionSpec as P

MESH = pl.DeviceIdType.MESH
BF = jnp.bfloat16
F32 = jnp.float32
EPSILON = 1e-05
LOG2E = 1.4426950408889634

N_GX, N_GY, N_GZ = 8, 4, 8
SLOT_CAP, OWN = 8, 4
F, J, HID = 64, 128, 256

ROWS = (432, 384)
LAYER_ROW = ((0, 96, 160, 224, 288, 368), (0, 64, 128, 192, 256, 320))
BELOW, MIDDLE, ABOVE = 64, 80, 352

SHARE_FROM = {1: (0, 6), -1: (1, 7), 2: (1, 4), -2: (3, 6), 3: (2, 2), -3: (5, 5)}
HOPS = ((-1, 0), (1, 0), (0, -1), (0, 1), (-1, -1), (1, -1), (-1, 1), (1, 1))

SEM_SHARE, SEM_HOP, SEM_DEPTH, SEM_HOME, SEM_COUNT = 0, 6, 22, 34, 40


def within(value, low, high):
    return jnp.logical_and(value >= low, value <= high)


def kernel(
    features, positions, counts, old_cuts, new_cuts, rates, conv_w, up_w, up_b, down_w, down_b,
    out,
    masked, places, parcel, shared, tile, column0, column1, low_halo, near, own, acc, bias_up,
    bias_down, home, send_sem, recv_sem,
):
    gx, gy, gz = lax.axis_index("gx"), lax.axis_index("gy"), lax.axis_index("gz")
    columns = (column0, column1)

    def copy(source, target, number, device):
        return pltpu.make_async_remote_copy(
            src_ref=source, dst_ref=target, send_sem=send_sem.at[number],
            recv_sem=recv_sem.at[number], device_id=device, device_id_type=MESH,
        )

    def has(dx, dy, dz):
        x, y, z = gx + dx, gy + dy, gz + dz
        ok = within(x, 0, N_GX - 1)
        ok = jnp.logical_and(ok, within(y, 0, N_GY - 1))
        return jnp.logical_and(ok, within(z, 0, N_GZ - 1))

    def paired(d):
        low, high = SHARE_FROM[d]
        return within(gx, low, high)

    partners = [((d, 0, 0), paired(d)) for d in SHARE_FROM]
    partners += [((dx, dy, 0), has(dx, dy, 0)) for dx, dy in HOPS if dy]
    partners += [((0, 0, dz), has(0, 0, dz)) for dz in (-1, 1)]

    for phase in range(2):
        cells = columns[phase]
        edge = 80 if phase == 0 else 64

        @pl.when(gx == 0)
        def _():
            for y in range(3):
                cells[1, y, :edge, :] = jnp.zeros((edge, J), BF)

        @pl.when(gx == N_GX - 1)
        def _():
            for y in range(3):
                cells[1, y, ROWS[phase] - edge :, :] = jnp.zeros((edge, J), BF)

        @pl.when(gy == 0)
        def _():
            cells[1, 0] = jnp.zeros((ROWS[phase], J), BF)

        @pl.when(gy == N_GY - 1)
        def _():
            cells[1, 2] = jnp.zeros((ROWS[phase], J), BF)

        @pl.when(gz == 0)
        def _():
            cells[0] = jnp.zeros((3, ROWS[phase], J), BF)

        @pl.when(gz == N_GZ - 1)
        def _():
            cells[2] = jnp.zeros((3, ROWS[phase], J), BF)

    barrier = pltpu.get_barrier_semaphore()
    for (dx, dy, dz), there in partners:

        @pl.when(there)
        def _():
            pl.semaphore_signal(
                barrier, inc=1, device_id=(gx + dx, gy + dy, gz + dz), device_id_type=MESH
            )

    particle = lax.broadcasted_iota(jnp.int32, (1, J), 1)
    for slot in range(SLOT_CAP):
        live = (particle < counts[slot]).astype(F32)
        masked[slot] = (features[slot].astype(F32) * live).astype(BF)
        places[slot, 0:3, :] = positions[slot].astype(F32)
        places[slot, 3:4, :] = live

    for d in (0, 1, -1, 2, -2, 3, -3):
        into = shared if d == 0 else parcel

        def pack():
            for t in range(OWN):
                slot = jnp.clip((gx + d) * OWN + t - old_cuts[gx], 0, SLOT_CAP - 1)
                into[d + 3, 16 + F * t : 16 + F * (t + 1), :] = masked[slot]
                tile[4 * t : 4 * t + 4, :] = places[slot, 0:4, :]
            into[d + 3, 0:16, :] = tile[...].astype(BF)

        if d == 0:
            pack()
        else:
            pl.when(paired(d))(pack)

    peers = jnp.int32(0)
    for _, there in partners:
        peers = peers + jnp.where(there, 1, 0)
    pl.semaphore_wait(barrier, peers)

    def share_copy(d):
        return copy(
            parcel.at[d + 3], shared.at[d + 3], SEM_SHARE + (d + 3 if d < 0 else d + 2),
            (gx + d, gy, gz),
        )

    for d in SHARE_FROM:
        pl.when(paired(d))(lambda d=d: share_copy(d).start())

    for layer in range(2):
        for half in range(2):
            row = up_b[layer : layer + 1, J * half : J * (half + 1)]
            bias_up[layer, J * half : J * (half + 1), :] = jnp.broadcast_to(row, (J, J)).T
        row = down_b[layer : layer + 1, :]
        row = jnp.concatenate([row, row], axis=1)
        bias_down[layer] = jnp.broadcast_to(row, (J, J)).T[:F]

    for d in SHARE_FROM:
        low, high = SHARE_FROM[d]
        pl.when(within(gx - d, low, high))(lambda d=d: share_copy(d).wait_recv())

    for t in range(OWN):
        place = gx * OWN + t
        holder = jnp.int32(0)
        for k in range(1, N_GX):
            holder = holder + jnp.where(old_cuts[k] <= place, 1, 0)
        came = jnp.clip(gx - holder + 3, 0, 6)
        row = LAYER_ROW[0][t + 1]
        column0[1, 1, row : row + F, :] = shared[came, 16 + F * t : 16 + F * (t + 1), :]
        tile[4 * t : 4 * t + 4, :] = shared[came, 0:16, :].astype(F32)[4 * t : 4 * t + 4]
    column0[1, 1, MIDDLE : MIDDLE + 16, :] = tile[...].astype(BF)
    low_halo[0:F, :] = column0[1, 1, LAYER_ROW[0][4] : LAYER_ROW[0][4] + F, :]
    low_halo[F : F + 16, :] = tile[...].astype(BF)

    def hop_copy(phase, number):
        dx, dy = HOPS[number]
        cells, at, y = columns[phase], LAYER_ROW[phase], 1 - dy
        if dx == 0:
            first = MIDDLE if phase == 0 else at[1]
            rows = pl.ds(first, at[4] + F - first)
            source, target = cells.at[1, 1, rows], cells.at[1, y, rows]
        elif dx == 1:
            if phase == 0:
                source, target = low_halo, cells.at[1, y, pl.ds(0, 80)]
            else:
                source, target = cells.at[1, 1, pl.ds(at[4], F)], cells.at[1, y, pl.ds(0, F)]
        else:
            if phase == 0:
                source = cells.at[1, 1, pl.ds(MIDDLE, 80)]
                target = cells.at[1, y, pl.ds(ABOVE, 80)]
            else:
                source, target = cells.at[1, 1, pl.ds(at[1], F)], cells.at[1, y, pl.ds(at[5], F)]
        return copy(source, target, SEM_HOP + 8 * phase + number, (gx + dx, gy + dy, gz))

    def depth_copy(phase, dz, y):
        cells = columns[phase]
        number = SEM_DEPTH + 6 * phase + 3 * (dz > 0) + y
        return copy(cells.at[1, y], cells.at[1 - dz, y], number, (gx, gy, gz + dz))

    def receive_hops(phase, numbers):
        for number in numbers:
            dx, dy = HOPS[number]
            pl.when(has(-dx, -dy, 0))(lambda n=number: hop_copy(phase, n).wait_recv())

    def send_depth(phase, y):
        for dz in (-1, 1):
            pl.when(has(0, 0, dz))(lambda dz=dz: depth_copy(phase, dz, y).start())

    def receive_depth(phase, y):
        for dz in (-1, 1):
            pl.when(has(0, 0, -dz))(lambda dz=dz: depth_copy(phase, dz, y).wait_recv())

    def locate(z, y):
        step = lax.broadcasted_iota(jnp.int32, (4, J), 0)
        middle = column0[z, y, MIDDLE : MIDDLE + 16, :].astype(F32)
        below = column0[z, y, BELOW : BELOW + 16, :].astype(F32)
        above = column0[z, y, ABOVE : ABOVE + 16, :].astype(F32)
        rows = [below[12:16]] + [middle[4 * t : 4 * t + 4] for t in range(OWN)] + [above[0:4]]
        for l in range(OWN + 2):
            shift = jnp.where(step == 0, float(l), jnp.where(step == 1, y - 1.0, z - 1.0))
            near[z, y, l, 0:4, :] = rows[l] - shift

    def convolve(phase, cells_of, first):
        cells, at = columns[phase], LAYER_ROW[phase]
        scale = [rates[phase, m] * -LOG2E for m in range(2)]
        beside = [(z, y, s) for z, y in cells_of for s in range(3)]

        def one_bin(b, carry):
            if first:
                total = [jnp.zeros((J, F), F32) for m in range(2)]
            else:
                total = [acc[b, m] for m in range(2)]
            for g in range(0, len(beside), 2):
                group = beside[g : g + 2]
                h, kern = [], [[], []]
                for z, y, s in group:
                    if phase == 0:
                        start = (b + s) * F + 16 * jnp.where(b + s > 0, 2, 0)
                        start = start + jnp.where(b + s > 4, 16, 0)
                    else:
                        start = (b + s) * F
                    h.append(cells[z, y, pl.ds(pl.multiple_of(start, 16), F), :])
                    dist = None
                    for c in range(3):
                        r = own[b, c] - near[z, y, b + s, c : c + 1, :]
                        dist = r * r if dist is None else dist + r * r
                    for m in range(2):
                        kern[m].append(jnp.exp2(dist * scale[m]).astype(BF))
                h = jnp.concatenate(h, axis=1)
                for m in range(2):
                    total[m] = total[m] + lax.dot_general(
                        jnp.concatenate(kern[m], axis=1), h, (((1,), (1,)), ((), ())),
                        preferred_element_type=F32,
                    )
            for m in range(2):
                acc[b, m] = total[m]
            return carry

        lax.fori_loop(0, OWN, one_bin, 0)

    def update(phase, b):
        gathered = jnp.concatenate([acc[b, 0], acc[b, 1]], axis=1).astype(BF)
        mixed = lax.dot_general(
            conv_w[phase], gathered, (((1,), (1,)), ((), ())), preferred_element_type=F32
        )
        centred = mixed - jnp.mean(mixed, axis=0, keepdims=True)
        spread = jnp.mean(centred * centred, axis=0, keepdims=True)
        normed = (centred * lax.rsqrt(spread + EPSILON)).astype(BF)
        raised = jnp.dot(up_w[phase], normed, preferred_element_type=F32) + bias_up[phase]
        hidden = jax.nn.silu(raised).astype(BF)
        change = jnp.dot(down_w[phase], hidden, preferred_element_type=F32) + bias_down[phase]
        row = LAYER_ROW[phase][b + 1]
        before = columns[phase][1, 1, row : row + F, :].astype(F32)
        live = near[1, 1, b + 1, 3:4, :]
        return ((before + change) * live).astype(BF)

    def layer(phase):
        for number in range(8):
            dx, dy = HOPS[number]
            pl.when(has(dx, dy, 0))(lambda n=number: hop_copy(phase, n).start())
        if phase == 0:
            for b in range(OWN):
                for c in range(3):
                    row = tile[4 * b + c : 4 * b + c + 1, :]
                    row = row - float(b + 1) if c == 0 else row
                    own[b, c] = jnp.broadcast_to(row, (J, J)).T
        receive_hops(phase, (0, 1))
        send_depth(phase, 1)
        if phase == 0:
            locate(1, 1)
        convolve(phase, [(1, 1)], True)
        receive_depth(phase, 1)
        if phase == 0:
            locate(0, 1)
            locate(2, 1)
        convolve(phase, [(0, 1), (2, 1)], False)
        receive_hops(phase, (3, 4 + 2, 4 + 3))
        send_depth(phase, 0)
        receive_hops(phase, (2, 4 + 0, 4 + 1))
        send_depth(phase, 2)
        if phase == 0:
            locate(1, 0)
            locate(1, 2)
        convolve(phase, [(1, 0), (1, 2)], False)
        receive_depth(phase, 0)
        if phase == 0:
            locate(0, 0)
            locate(2, 0)
        convolve(phase, [(0, 0), (2, 0)], False)
        receive_depth(phase, 2)
        if phase == 0:
            locate(0, 2)
            locate(2, 2)
        convolve(phase, [(0, 2), (2, 2)], False)

    layer(0)
    for b in range(OWN):
        row = LAYER_ROW[1][b + 1]
        column1[1, 1, row : row + F, :] = update(0, b)
    layer(1)
    for b in range(OWN):
        home[gx * OWN + b] = update(1, b)

    def home_copy(d):
        rows = home.at[pl.ds(gx * OWN, OWN)]
        return copy(rows, rows, SEM_HOME + (d + 3 if d < 0 else d + 2), (gx + d, gy, gz))

    for d in SHARE_FROM:
        pl.when(paired(d))(lambda d=d: home_copy(d).start())
    for d in SHARE_FROM:
        low, high = SHARE_FROM[d]

        @pl.when(within(gx - d, low, high))
        def _():
            rows = home.at[pl.ds((gx - d) * OWN, OWN)]
            copy(
                rows, rows, SEM_HOME + (d + 3 if d < 0 else d + 2), (gx + d, gy, gz)
            ).wait_recv()

    held = new_cuts[gx + 1] - new_cuts[gx]
    for slot in range(SLOT_CAP):
        place = jnp.clip(new_cuts[gx] + slot, 0, N_GX * OWN - 1)
        keep = jnp.broadcast_to(held, (F, J)) > slot
        out[slot] = jnp.where(keep, home[place].astype(F32), 0.0).astype(BF)

    for d in SHARE_FROM:
        pl.when(paired(d))(lambda d=d: share_copy(d).wait_send())
        pl.when(paired(d))(lambda d=d: home_copy(d).wait_send())
    for phase in range(2):
        for number in range(8):
            dx, dy = HOPS[number]
            pl.when(has(dx, dy, 0))(lambda n=number: hop_copy(phase, n).wait_send())
        for dz in (-1, 1):
            for y in range(3):
                pl.when(has(0, 0, dz))(lambda dz=dz, y=y: depth_copy(phase, dz, y).wait_send())


def local(
    features, positions, counts, old_cuts, new_cuts, radial_rates, conv_weight, up_weight, up_bias,
    down_weight, down_bias,
):
    smem = pl.BlockSpec(memory_space=pltpu.SMEM)
    vmem = pl.BlockSpec(memory_space=pltpu.VMEM)
    result = pl.pallas_call(
        kernel,
        out_shape=jax.ShapeDtypeStruct((SLOT_CAP, F, J), BF),
        in_specs=[vmem, vmem, smem, smem, smem, smem, vmem, vmem, vmem, vmem, vmem],
        out_specs=vmem,
        scratch_shapes=[
            pltpu.VMEM((SLOT_CAP, F, J), BF),
            pltpu.VMEM((SLOT_CAP, 8, J), F32),
            pltpu.VMEM((7, 272, J), BF),
            pltpu.VMEM((7, 272, J), BF),
            pltpu.VMEM((16, J), F32),
            pltpu.VMEM((3, 3, ROWS[0], J), BF),
            pltpu.VMEM((3, 3, ROWS[1], J), BF),
            pltpu.VMEM((80, J), BF),
            pltpu.VMEM((3, 3, OWN + 2, 8, J), F32),
            pltpu.VMEM((OWN, 3, J, J), F32),
            pltpu.VMEM((OWN, 2, J, F), F32),
            pltpu.VMEM((2, HID, J), F32),
            pltpu.VMEM((2, F, J), F32),
            pltpu.VMEM((N_GX * OWN, F, J), BF),
            pltpu.SemaphoreType.DMA((SEM_COUNT,)),
            pltpu.SemaphoreType.DMA((SEM_COUNT,)),
        ],
        compiler_params=pltpu.CompilerParams(
            collective_id=0, has_side_effects=True, vmem_limit_bytes=32 * 2**20
        ),
    )(
        features.reshape(SLOT_CAP, F, J),
        positions.reshape(SLOT_CAP, 3, J),
        counts.reshape(SLOT_CAP),
        old_cuts,
        new_cuts,
        radial_rates,
        conv_weight.reshape(2, F, 2 * F),
        up_weight,
        up_bias,
        down_weight,
        down_bias,
    )
    return result.reshape(SLOT_CAP, 1, 1, F, J)


def solution(mesh):
    grid = P("gx", "gy", "gz")
    return jax.shard_map(
        local,
        mesh=mesh,
        in_specs=(grid, grid, grid) + (P(),) * 8,
        out_specs=grid,
        check_vma=False,
    )
```

```python
import jax
import jax.numpy as jnp
from jax import lax
from jax.experimental import pallas as pl
from jax.experimental.pallas import tpu as pltpu
from jax.sharding import PartitionSpec as P

MESH = pl.DeviceIdType.MESH
BF = jnp.bfloat16
F32 = jnp.float32
EPSILON = 1e-05
LOG2E = 1.4426950408889634

N_GX, N_GY, N_GZ = 8, 4, 8
SLOT_CAP, OWN = 8, 4
F, J, HID = 64, 128, 256

COLUMN = 432
ROW = (352, 16, 80, 144, 208, 288)
TILE, TILE_ABOVE, TILE_BELOW = 0, 272, 416
PARCEL = 272

SHARE_FROM = {0: (0, 7), 1: (0, 6), -1: (1, 7), 2: (1, 4), -2: (3, 6), 3: (2, 2), -3: (5, 5)}
ENDS = (-1, 1)
CORNERS = ((-1, -1), (1, -1), (-1, 1), (1, 1))
PARTS = (((0, 272),), ((80, 128), (16, 64), (208, 64)))
HOME = ((1, 2), (0, 1), (3, 1))


def name_copies():
    names = [("share", d) for d in SHARE_FROM]
    for phase in range(2):
        names += [("x", phase, dx) for dx in ENDS]
        names += [("xy", phase, dx, dy) for dx, dy in CORNERS]
        for part in range(len(PARTS[phase])):
            names += [("y", phase, dy, part) for dy in ENDS]
            names += [("z", phase, dz, y, part) for dz in ENDS for y in range(3)]
        names += [("zx", phase, dz, y) for dz in ENDS for y in range(3)]
    names += [("home", d, part) for d in SHARE_FROM for part in range(len(HOME))]
    return {name: number for number, name in enumerate(names)}


NUMBER = name_copies()


def snake(k):
    return k + ((k // 2) % 2) * (1 - 2 * (k % 2))


def gx_partners():
    met = {k: set() for k in range(N_GX)}
    for d, (low, high) in SHARE_FROM.items():
        for k in range(low, high + 1):
            met[k].add(snake(k + d))
            met[snake(k + d)].add(k)
    for s in range(N_GX - 1):
        met[snake(s)].add(snake(s + 1))
        met[snake(s + 1)].add(snake(s))
    return {j: sorted(k for k in met if j in met[k] and j != k) for j in range(N_GX)}


def within(value, low, high):
    return jnp.logical_and(value >= low, value <= high)


def either(conditions):
    result = conditions[0]
    for condition in conditions[1:]:
        result = jnp.logical_or(result, condition)
    return result


def kernel(
    features_in, positions_in, counts_in, old_cuts_in, new_cuts_in, rates_in, conv_w_in, up_w_in,
    up_b_in, down_w_in, down_b_in,
    out,
    features, positions, counts, old_cuts, new_cuts, rates, conv_w, up_w_read, up_b, down_w, down_b,
    up_w, masked, places, parcel, shared, tile, column0, column1, low_halo, near, own, acc, bias_up,
    bias_down, home, load_sem, send_sem, recv_sem,
):
    gx, gy, gz = lax.axis_index("gx"), lax.axis_index("gy"), lax.axis_index("gz")
    share = snake(gx)
    columns = (column0, column1)

    def keeper(s):
        return snake(jnp.clip(s, 0, N_GX - 1))

    def copy(name, source, target, device):
        return pltpu.make_async_remote_copy(
            src_ref=source, dst_ref=target, send_sem=send_sem.at[NUMBER[name]],
            recv_sem=recv_sem.at[NUMBER[name]], device_id=device, device_id_type=MESH,
        )

    def has(dx, dy, dz):
        ok = None
        for place, count, step in ((share, N_GX, dx), (gy, N_GY, dy), (gz, N_GZ, dz)):
            if step:
                here = place < count - 1 if step > 0 else place > 0
                ok = here if ok is None else jnp.logical_and(ok, here)
        return ok

    for cells in columns:

        @pl.when(share == 0)
        def _():
            for y in range(3):
                cells[1, y, ROW[0] : ROW[0] + 80, :] = jnp.zeros((80, J), BF)

        @pl.when(share == N_GX - 1)
        def _():
            for y in range(3):
                cells[1, y, TILE_ABOVE : TILE_ABOVE + 80, :] = jnp.zeros((80, J), BF)

        @pl.when(gy == 0)
        def _():
            cells[1, 0] = jnp.zeros((COLUMN, J), BF)

        @pl.when(gy == N_GY - 1)
        def _():
            cells[1, 2] = jnp.zeros((COLUMN, J), BF)

        @pl.when(gz == 0)
        def _():
            cells[0] = jnp.zeros((3, COLUMN, J), BF)

        @pl.when(gz == N_GZ - 1)
        def _():
            cells[2] = jnp.zeros((3, COLUMN, J), BF)

    partners = []
    for j, near_j in gx_partners().items():
        partners.append(((j, gy, gz), either([gx == k for k in near_j])))
    for dx, dy in CORNERS:
        partners.append(((keeper(share + dx), gy + dy, gz), has(dx, dy, 0)))
    for step in ENDS:
        partners.append(((gx, gy + step, gz), has(0, step, 0)))
        partners.append(((gx, gy, gz + step), has(0, 0, step)))
    barrier = pltpu.get_barrier_semaphore()
    peers = jnp.int32(0)
    for device, there in partners:
        peers = peers + jnp.where(there, 1, 0)

        @pl.when(there)
        def _():
            pl.semaphore_signal(barrier, inc=1, device_id=device, device_id_type=MESH)

    arguments = (
        (counts_in, counts), (old_cuts_in, old_cuts), (features_in, features),
        (positions_in, positions), (up_b_in, up_b), (down_b_in, down_b), (up_w_in, up_w_read),
        (conv_w_in, conv_w), (down_w_in, down_w), (rates_in, rates), (new_cuts_in, new_cuts),
    )
    loads = [
        pltpu.make_async_copy(source, target, load_sem.at[n])
        for n, (source, target) in enumerate(arguments)
    ]
    for load in loads:
        load.start()
    for load in loads[:4]:
        load.wait()

    particle = lax.broadcasted_iota(jnp.int32, (1, J), 1)
    for slot in range(SLOT_CAP):
        live = (particle < counts[slot]).astype(F32)
        masked[slot] = (features[slot].astype(F32) * live).astype(BF)
        for c in range(3):
            places[slot, c : c + 1, :] = positions[c].astype(F32)[slot : slot + 1, :]
        places[slot, 3:4, :] = live

    def share_sent(d):
        low, high = SHARE_FROM[d]
        return within(gx, low, high), keeper(gx + d)

    def share_came(d):
        low, high = SHARE_FROM[d]
        return jnp.logical_and(within(share - d, low, high), share - d != gx)

    def share_copy(d):
        return copy(
            ("share", d), parcel.at[d + 3], shared.at[d + 3], (share_sent(d)[1], gy, gz)
        )

    for d in SHARE_FROM:
        used, device = share_sent(d)

        @pl.when(used)
        def _():
            for t in range(OWN):
                slot = jnp.clip((gx + d) * OWN + t - old_cuts[gx], 0, SLOT_CAP - 1)
                parcel[d + 3, 16 + F * t : 16 + F * (t + 1), :] = masked[slot]
                tile[4 * t : 4 * t + 4, :] = places[slot, 0:4, :]
            parcel[d + 3, 0:16, :] = tile[...].astype(BF)

        @pl.when(jnp.logical_and(used, device == gx))
        def _():
            shared[d + 3] = parcel[d + 3]

    pl.semaphore_wait(barrier, peers)

    for d in SHARE_FROM:
        used, device = share_sent(d)
        pl.when(jnp.logical_and(used, device != gx))(lambda d=d: share_copy(d).start())
    for load in loads[4:]:
        load.wait()
    for phase in range(2):
        for half in range(2):
            row = up_b[phase : phase + 1, J * half : J * (half + 1)]
            bias_up[phase, J * half : J * (half + 1), :] = jnp.broadcast_to(row, (J, J)).T
        row = down_b[phase : phase + 1, :]
        row = jnp.concatenate([row, row], axis=1)
        bias_down[phase] = jnp.broadcast_to(row, (J, J)).T[:F]
        up_w[phase] = up_w_read[phase].astype(F32).T.astype(BF)

    for d in SHARE_FROM:
        pl.when(share_came(d))(lambda d=d: share_copy(d).wait_recv())

    for t in range(OWN):
        place = share * OWN + t
        holder = jnp.int32(0)
        for k in range(1, N_GX):
            holder = holder + jnp.where(old_cuts[k] <= place, 1, 0)
        came = jnp.clip(share - holder + 3, 0, 6)
        column0[1, 1, ROW[t + 1] : ROW[t + 1] + F, :] = shared[came, 16 + F * t : 16 + F * (t + 1), :]
        tile[4 * t : 4 * t + 4, :] = shared[came, 0:16, :].astype(F32)[4 * t : 4 * t + 4]
    column0[1, 1, 0:16, :] = tile[...].astype(BF)
    low_halo[0:F, :] = column0[1, 1, ROW[4] : ROW[4] + F, :]
    low_halo[F : F + 16, :] = tile[...].astype(BF)

    def x_copy(phase, dx, dy):
        cells, y = columns[phase], 1 - dy
        extra = 16 if phase == 0 else 0
        if dx == 1:
            source = low_halo if phase == 0 else cells.at[1, 1, pl.ds(ROW[4], F)]
            target = cells.at[1, y, pl.ds(ROW[0], F + extra)]
        else:
            source = cells.at[1, 1, pl.ds(ROW[1] - extra, F + extra)]
            target = cells.at[1, y, pl.ds(ROW[5] - extra, F + extra)]
        name = ("xy", phase, dx, dy) if dy else ("x", phase, dx)
        return copy(name, source, target, (keeper(share + dx), gy + dy, gz))

    def y_copy(phase, dy, part):
        cells, rows = columns[phase], pl.ds(*PARTS[phase][part])
        return copy(
            ("y", phase, dy, part), cells.at[1, 1, rows], cells.at[1, 1 - dy, rows],
            (gx, gy + dy, gz),
        )

    def z_copy(phase, dz, y, part):
        cells, rows = columns[phase], pl.ds(*PARTS[phase][part])
        return copy(
            ("z", phase, dz, y, part), cells.at[1, y, rows], cells.at[1 - dz, y, rows],
            (gx, gy, gz + dz),
        )

    def zx_copy(phase, dz, y):
        cells, rows = columns[phase], pl.ds(TILE_ABOVE, 160) if phase == 0 else pl.ds(ROW[5], 128)
        return copy(
            ("zx", phase, dz, y), cells.at[1, y, rows], cells.at[1 - dz, y, rows],
            (gx, gy, gz + dz),
        )

    def locate(z, y, inner):
        step = lax.broadcasted_iota(jnp.int32, (4, J), 0)
        if inner:
            rows = column0[z, y, TILE : TILE + 16, :].astype(F32)
            rows = {t + 1: rows[4 * t : 4 * t + 4] for t in range(OWN)}
        else:
            below = column0[z, y, TILE_BELOW : TILE_BELOW + 16, :].astype(F32)
            above = column0[z, y, TILE_ABOVE : TILE_ABOVE + 16, :].astype(F32)
            rows = {0: below[12:16], 5: above[0:4]}
        for l, row in rows.items():
            shift = jnp.where(step == 0, float(l), jnp.where(step == 1, y - 1.0, z - 1.0))
            near[z, y, l, 0:4, :] = row - shift

    begun = set()

    def convolve(phase, cells_of, inner):
        cells = columns[phase]
        scale = [rates[phase, m] * -LOG2E for m in range(2)]
        for b in range(OWN) if inner else (0, 3):
            wanted = range(max(b, 1), min(b + 2, 4) + 1) if inner else (0,) if b == 0 else (5,)
            beside = [(z, y, l) for l in wanted for z, y in cells_of]
            if (phase, b) in begun:
                total = [acc[b, m] for m in range(2)]
            else:
                total = [jnp.zeros((J, F), F32) for m in range(2)]
                begun.add((phase, b))
            for g in range(0, len(beside), 2):
                h, kern = [], [[], []]
                for z, y, l in beside[g : g + 2]:
                    h.append(cells[z, y, ROW[l] : ROW[l] + F, :])
                    dist = None
                    for c in range(3):
                        r = own[b, c] - near[z, y, l, c : c + 1, :]
                        dist = r * r if dist is None else dist + r * r
                    for m in range(2):
                        kern[m].append(jnp.exp2(dist * scale[m]).astype(BF))
                h = jnp.concatenate(h, axis=1)
                for m in range(2):
                    total[m] = total[m] + lax.dot_general(
                        jnp.concatenate(kern[m], axis=1), h, (((1,), (1,)), ((), ())),
                        preferred_element_type=F32,
                    )
            for m in range(2):
                acc[b, m] = total[m]

    def update(phase, bins):
        gathered = [jnp.concatenate([acc[b, m] for b in bins], axis=0).astype(BF) for m in range(2)]
        mixed = None
        for m in range(2):
            term = lax.dot_general(
                conv_w[phase, :, m, :], gathered[m], (((1,), (1,)), ((), ())),
                preferred_element_type=F32,
            )
            mixed = term if mixed is None else mixed + term
        centred = mixed - jnp.mean(mixed, axis=0, keepdims=True)
        spread = jnp.mean(centred * centred, axis=0, keepdims=True)
        normed = (centred * lax.rsqrt(spread + EPSILON)).astype(BF)
        raised = jnp.dot(up_w[phase], normed, preferred_element_type=F32)
        raised = raised + jnp.concatenate([bias_up[phase]] * 2, axis=1)
        hidden = jax.nn.silu(raised).astype(BF)
        change = jnp.dot(down_w[phase], hidden, preferred_element_type=F32)
        change = change + jnp.concatenate([bias_down[phase]] * 2, axis=1)
        for n, b in enumerate(bins):
            before = columns[phase][1, 1, ROW[b + 1] : ROW[b + 1] + F, :].astype(F32)
            live = near[1, 1, b + 1, 3:4, :]
            after = ((before + change[:, J * n : J * (n + 1)]) * live).astype(BF)
            if phase == 0:
                column1[1, 1, ROW[b + 1] : ROW[b + 1] + F, :] = after
            else:
                home[share * OWN + b] = after

    def home_copy(d, part):
        first, count = HOME[part]
        rows = home.at[pl.ds(share * OWN + first, count)]
        return copy(("home", d, part), rows, rows, (share - d, gy, gz))

    def start_own(phase, parts):
        for part in parts:
            for dz in ENDS:
                pl.when(has(0, 0, dz))(lambda dz=dz, p=part: z_copy(phase, dz, 1, p).start())
            for dy in ENDS:
                pl.when(has(0, dy, 0))(lambda dy=dy, p=part: y_copy(phase, dy, p).start())

    def start_halo(phase):
        for dx in ENDS:
            pl.when(has(dx, 0, 0))(lambda dx=dx: x_copy(phase, dx, 0).start())
        for dx, dy in CORNERS:
            pl.when(has(dx, dy, 0))(lambda dx=dx, dy=dy: x_copy(phase, dx, dy).start())

    def start_home(parts):
        for part in parts:
            for d in SHARE_FROM:
                pl.when(share_came(d))(lambda d=d, p=part: home_copy(d, p).start())

    def forward(phase, y, part):
        dy = 1 - y
        pl.when(has(0, -dy, 0))(lambda: y_copy(phase, dy, part).wait_recv())
        for dz in ENDS:
            pl.when(has(0, 0, dz))(lambda dz=dz: z_copy(phase, dz, y, part).start())

    def forward_halo(phase, y):
        dy = 1 - y
        for dx in ENDS:
            pl.when(has(-dx, -dy, 0))(lambda dx=dx: x_copy(phase, dx, dy).wait_recv())
        for dz in ENDS:
            pl.when(has(0, 0, dz))(lambda dz=dz: zx_copy(phase, dz, y).start())

    def receive_z(phase, y, part):
        for dz in ENDS:
            pl.when(has(0, 0, -dz))(lambda dz=dz: z_copy(phase, dz, y, part).wait_recv())

    def receive_zx(phase, y):
        for dz in ENDS:
            pl.when(has(0, 0, -dz))(lambda dz=dz: zx_copy(phase, dz, y).wait_recv())

    def find(phase, cells_of, inner):
        if phase == 0:
            for z, y in cells_of:
                locate(z, y, inner)

    def layer(phase):
        parts = range(len(PARTS[phase]))
        sides, beside = [(0, 1), (2, 1)], [(1, 0), (1, 2)]
        start_halo(phase)
        start_own(phase, parts if phase == 0 else parts[1:])
        if phase == 0:
            for b in range(OWN):
                for c in range(3):
                    row = tile[4 * b + c : 4 * b + c + 1, :]
                    row = row - float(b + 1) if c == 0 else row
                    own[b, c] = jnp.broadcast_to(row, (J, J)).T
        find(phase, [(1, 1)], True)
        convolve(phase, [(1, 1)], True)
        forward_halo(phase, 1)
        find(phase, [(1, 1)], False)
        convolve(phase, [(1, 1)], False)
        if phase == 1:
            forward(phase, 0, 0)
            forward(phase, 2, 0)
        for part in parts:
            receive_z(phase, 1, part)
        find(phase, sides, True)
        convolve(phase, sides, True)
        for part in parts[phase:]:
            forward(phase, 0, part)
            forward(phase, 2, part)
        find(phase, beside, True)
        convolve(phase, beside, True)
        forward_halo(phase, 0)
        forward_halo(phase, 2)
        receive_zx(phase, 1)
        find(phase, sides, False)
        convolve(phase, sides, False)
        find(phase, beside, False)
        convolve(phase, beside, False)
        for y in (0, 2):
            for part in parts:
                receive_z(phase, y, part)
            find(phase, [(0, y), (2, y)], True)
            convolve(phase, [(0, y), (2, y)], True)
        update(phase, (1, 2))
        if phase == 0:
            start_own(1, (0,))
        else:
            start_home((0,))
        for y in (0, 2):
            receive_zx(phase, y)
            find(phase, [(0, y), (2, y)], False)
            convolve(phase, [(0, y), (2, y)], False)
        update(phase, (0, 3))

    layer(0)
    layer(1)
    start_home((1, 2))

    for d in SHARE_FROM:
        used, device = share_sent(d)

        @pl.when(jnp.logical_and(used, device != gx))
        def _():
            for part, (first, count) in enumerate(HOME):
                rows = home.at[pl.ds((gx + d) * OWN + first, count)]
                copy(("home", d, part), rows, rows, (device, gy, gz)).wait_recv()

    held = new_cuts[gx + 1] - new_cuts[gx]
    for slot in range(SLOT_CAP):
        place = jnp.clip(new_cuts[gx] + slot, 0, N_GX * OWN - 1)
        keep = jnp.broadcast_to(held, (F, J)) > slot
        out[slot] = jnp.where(keep, home[place].astype(F32), 0.0).astype(BF)

    for d in SHARE_FROM:
        used, device = share_sent(d)
        pl.when(jnp.logical_and(used, device != gx))(lambda d=d: share_copy(d).wait_send())
        for part in range(len(HOME)):
            pl.when(share_came(d))(lambda d=d, p=part: home_copy(d, p).wait_send())
    for phase in range(2):
        for dx in ENDS:
            for dy in (-1, 0, 1):
                pl.when(has(dx, dy, 0))(lambda dx=dx, dy=dy: x_copy(phase, dx, dy).wait_send())
        for part in range(len(PARTS[phase])):
            for dy in ENDS:
                pl.when(has(0, dy, 0))(lambda dy=dy, p=part: y_copy(phase, dy, p).wait_send())
        for dz in ENDS:

            @pl.when(has(0, 0, dz))
            def _():
                for y in range(3):
                    zx_copy(phase, dz, y).wait_send()
                    for part in range(len(PARTS[phase])):
                        z_copy(phase, dz, y, part).wait_send()


def local(
    features, positions, counts, old_cuts, new_cuts, radial_rates, conv_weight, up_weight, up_bias,
    down_weight, down_bias,
):
    result = pl.pallas_call(
        kernel,
        out_shape=jax.ShapeDtypeStruct((SLOT_CAP, F, J), BF),
        in_specs=[pl.BlockSpec(memory_space=pl.ANY)] * 11,
        out_specs=pl.BlockSpec(memory_space=pltpu.VMEM),
        scratch_shapes=[
            pltpu.VMEM((SLOT_CAP, F, J), BF),
            pltpu.VMEM((3, SLOT_CAP, J), BF),
            pltpu.SMEM((SLOT_CAP,), jnp.int32),
            pltpu.SMEM((N_GX + 1,), jnp.int32),
            pltpu.SMEM((N_GX + 1,), jnp.int32),
            pltpu.SMEM((2, 2), F32),
            pltpu.VMEM((2, F, 2, F), BF),
            pltpu.VMEM((2, F, HID), BF),
            pltpu.VMEM((2, HID), F32),
            pltpu.VMEM((2, F, HID), BF),
            pltpu.VMEM((2, F), F32),
            pltpu.VMEM((2, HID, F), BF),
            pltpu.VMEM((SLOT_CAP, F, J), BF),
            pltpu.VMEM((SLOT_CAP, 8, J), F32),
            pltpu.VMEM((7, PARCEL, J), BF),
            pltpu.VMEM((7, PARCEL, J), BF),
            pltpu.VMEM((16, J), F32),
            pltpu.VMEM((3, 3, COLUMN, J), BF),
            pltpu.VMEM((3, 3, COLUMN, J), BF),
            pltpu.VMEM((80, J), BF),
            pltpu.VMEM((3, 3, OWN + 2, 8, J), F32),
            pltpu.VMEM((OWN, 3, J, J), F32),
            pltpu.VMEM((OWN, 2, J, F), F32),
            pltpu.VMEM((2, HID, J), F32),
            pltpu.VMEM((2, F, J), F32),
            pltpu.VMEM((N_GX * OWN, F, J), BF),
            pltpu.SemaphoreType.DMA((11,)),
            pltpu.SemaphoreType.DMA((len(NUMBER),)),
            pltpu.SemaphoreType.DMA((len(NUMBER),)),
        ],
        compiler_params=pltpu.CompilerParams(
            collective_id=0, has_side_effects=True, vmem_limit_bytes=60 * 2**20
        ),
    )(
        features.reshape(SLOT_CAP, F, J),
        positions.transpose(1, 2, 3, 0, 4).reshape(3, SLOT_CAP, J),
        counts.reshape(SLOT_CAP),
        old_cuts,
        new_cuts,
        radial_rates,
        conv_weight,
        up_weight.transpose(0, 2, 1),
        up_bias,
        down_weight,
        down_bias,
    )
    return result.reshape(SLOT_CAP, 1, 1, F, J)


def solution(mesh):
    grid = P("gx", "gy", "gz")
    return jax.shard_map(
        local,
        mesh=mesh,
        in_specs=(grid, grid, grid) + (P(),) * 8,
        out_specs=grid,
        check_vma=False,
    )
```

```python
import jax
import jax.numpy as jnp
from jax import lax
from jax.experimental import pallas as pl
from jax.experimental.pallas import tpu as pltpu
from jax.sharding import PartitionSpec as P

MESH = pl.DeviceIdType.MESH
BF = jnp.bfloat16
F32 = jnp.float32
EPSILON = 1e-05
LOG2E = 1.4426950408889634

N_GX, N_GY, N_GZ = 8, 4, 8
SLOT_CAP, OWN = 8, 4
F, J, HID = 64, 128, 256

COLUMN = 432
ROW = (352, 16, 80, 144, 208, 288)
TILE, TILE_ABOVE, TILE_BELOW = 0, 272, 416
PARCEL = 272

SHARE_FROM = {0: (0, 7), 1: (0, 6), -1: (1, 7), 2: (1, 4), -2: (3, 6), 3: (2, 2), -3: (5, 5)}
ENDS = (-1, 1)
CORNERS = ((-1, -1), (1, -1), (-1, 1), (1, 1))
PARTS = (((0, 272),), ((80, 128), (16, 64), (208, 64)))
HOME = ((1, 2), (0, 1), (3, 1))


def name_copies():
    names = [("share", d) for d in SHARE_FROM]
    for phase in range(2):
        names += [("x", phase, dx) for dx in ENDS]
        names += [("xy", phase, dx, dy) for dx, dy in CORNERS]
        for part in range(len(PARTS[phase])):
            names += [("y", phase, dy, part) for dy in ENDS]
            names += [("z", phase, dz, y, part) for dz in ENDS for y in range(3)]
        names += [("zx", phase, dz, y) for dz in ENDS for y in range(3)]
    names += [("home", d, part) for d in SHARE_FROM for part in range(len(HOME))]
    return {name: number for number, name in enumerate(names)}


NUMBER = name_copies()


def snake(k):
    return k + ((k // 2) % 2) * (1 - 2 * (k % 2))


def gx_partners():
    met = {k: set() for k in range(N_GX)}
    for d, (low, high) in SHARE_FROM.items():
        for k in range(low, high + 1):
            met[k].add(snake(k + d))
            met[snake(k + d)].add(k)
    for s in range(N_GX - 1):
        met[snake(s)].add(snake(s + 1))
        met[snake(s + 1)].add(snake(s))
    return {j: sorted(k for k in met if j in met[k] and j != k) for j in range(N_GX)}


def within(value, low, high):
    return jnp.logical_and(value >= low, value <= high)


def either(conditions):
    result = conditions[0]
    for condition in conditions[1:]:
        result = jnp.logical_or(result, condition)
    return result


def kernel(
    features_in, positions_in, counts_in, old_cuts_in, new_cuts_in, rates_in, conv_w_in, up_w_in,
    up_b_in, down_w_in, down_b_in,
    out,
    features, positions, counts, old_cuts, new_cuts, rates, conv_w, up_w_read, up_b, down_w, down_b,
    up_w, masked, places, parcel, shared, tile, column0, column1, low_halo, near, own, acc, bias_up,
    bias_down, home, load_sem, send_sem, recv_sem,
):
    gx, gy, gz = lax.axis_index("gx"), lax.axis_index("gy"), lax.axis_index("gz")
    share = snake(gx)
    columns = (column0, column1)

    def keeper(s):
        return snake(jnp.clip(s, 0, N_GX - 1))

    def copy(name, source, target, device):
        return pltpu.make_async_remote_copy(
            src_ref=source, dst_ref=target, send_sem=send_sem.at[NUMBER[name]],
            recv_sem=recv_sem.at[NUMBER[name]], device_id=device, device_id_type=MESH,
        )

    def has(dx, dy, dz):
        ok = None
        for place, count, step in ((share, N_GX, dx), (gy, N_GY, dy), (gz, N_GZ, dz)):
            if step:
                here = place < count - 1 if step > 0 else place > 0
                ok = here if ok is None else jnp.logical_and(ok, here)
        return ok

    for cells in columns:

        @pl.when(share == 0)
        def _():
            for y in range(3):
                cells[1, y, ROW[0] : ROW[0] + 80, :] = jnp.zeros((80, J), BF)

        @pl.when(share == N_GX - 1)
        def _():
            for y in range(3):
                cells[1, y, TILE_ABOVE : TILE_ABOVE + 80, :] = jnp.zeros((80, J), BF)

        @pl.when(gy == 0)
        def _():
            cells[1, 0] = jnp.zeros((COLUMN, J), BF)

        @pl.when(gy == N_GY - 1)
        def _():
            cells[1, 2] = jnp.zeros((COLUMN, J), BF)

        @pl.when(gz == 0)
        def _():
            cells[0] = jnp.zeros((3, COLUMN, J), BF)

        @pl.when(gz == N_GZ - 1)
        def _():
            cells[2] = jnp.zeros((3, COLUMN, J), BF)

    partners = []
    for j, near_j in gx_partners().items():
        partners.append(((j, gy, gz), either([gx == k for k in near_j])))
    for dx, dy in CORNERS:
        partners.append(((keeper(share + dx), gy + dy, gz), has(dx, dy, 0)))
    for step in ENDS:
        partners.append(((gx, gy + step, gz), has(0, step, 0)))
        partners.append(((gx, gy, gz + step), has(0, 0, step)))
    barrier = pltpu.get_barrier_semaphore()
    peers = jnp.int32(0)
    for device, there in partners:
        peers = peers + jnp.where(there, 1, 0)

        @pl.when(there)
        def _():
            pl.semaphore_signal(barrier, inc=1, device_id=device, device_id_type=MESH)

    arguments = (
        (counts_in, counts), (old_cuts_in, old_cuts), (features_in, features),
        (positions_in, positions), (up_b_in, up_b), (down_b_in, down_b), (up_w_in, up_w_read),
        (conv_w_in, conv_w), (down_w_in, down_w), (rates_in, rates), (new_cuts_in, new_cuts),
    )
    loads = [
        pltpu.make_async_copy(source, target, load_sem.at[n])
        for n, (source, target) in enumerate(arguments)
    ]
    for load in loads:
        load.start()
    for load in loads[:4]:
        load.wait()

    particle = lax.broadcasted_iota(jnp.int32, (1, J), 1)
    for slot in range(SLOT_CAP):
        live = (particle < counts[slot]).astype(F32)
        masked[slot] = (features[slot].astype(F32) * live).astype(BF)
        for c in range(3):
            places[slot, c : c + 1, :] = positions[c].astype(F32)[slot : slot + 1, :]
        places[slot, 3:4, :] = live

    def share_sent(d):
        low, high = SHARE_FROM[d]
        return within(gx, low, high), keeper(gx + d)

    def share_came(d):
        low, high = SHARE_FROM[d]
        return jnp.logical_and(within(share - d, low, high), share - d != gx)

    def share_copy(d):
        return copy(
            ("share", d), parcel.at[d + 3], shared.at[d + 3], (share_sent(d)[1], gy, gz)
        )

    for d in SHARE_FROM:
        used, device = share_sent(d)

        @pl.when(used)
        def _():
            for t in range(OWN):
                slot = jnp.clip((gx + d) * OWN + t - old_cuts[gx], 0, SLOT_CAP - 1)
                parcel[d + 3, 16 + F * t : 16 + F * (t + 1), :] = masked[slot]
                tile[4 * t : 4 * t + 4, :] = places[slot, 0:4, :]
            parcel[d + 3, 0:16, :] = tile[...].astype(BF)

        @pl.when(jnp.logical_and(used, device == gx))
        def _():
            shared[d + 3] = parcel[d + 3]

    pl.semaphore_wait(barrier, peers)

    for d in SHARE_FROM:
        used, device = share_sent(d)
        pl.when(jnp.logical_and(used, device != gx))(lambda d=d: share_copy(d).start())
    for load in loads[4:]:
        load.wait()
    for phase in range(2):
        for half in range(2):
            row = up_b[phase : phase + 1, J * half : J * (half + 1)]
            bias_up[phase, J * half : J * (half + 1), :] = jnp.broadcast_to(row, (J, J)).T
        row = down_b[phase : phase + 1, :]
        row = jnp.concatenate([row, row], axis=1)
        bias_down[phase] = jnp.broadcast_to(row, (J, J)).T[:F]
        up_w[phase] = up_w_read[phase].astype(F32).T.astype(BF)

    for d in SHARE_FROM:
        pl.when(share_came(d))(lambda d=d: share_copy(d).wait_recv())

    for t in range(OWN):
        place = share * OWN + t
        holder = jnp.int32(0)
        for k in range(1, N_GX):
            holder = holder + jnp.where(old_cuts[k] <= place, 1, 0)
        came = jnp.clip(share - holder + 3, 0, 6)
        column0[1, 1, ROW[t + 1] : ROW[t + 1] + F, :] = shared[came, 16 + F * t : 16 + F * (t + 1), :]
        tile[4 * t : 4 * t + 4, :] = shared[came, 0:16, :].astype(F32)[4 * t : 4 * t + 4]
    column0[1, 1, 0:16, :] = tile[...].astype(BF)
    low_halo[0:F, :] = column0[1, 1, ROW[4] : ROW[4] + F, :]
    low_halo[F : F + 16, :] = tile[...].astype(BF)

    def x_copy(phase, dx, dy):
        cells, y = columns[phase], 1 - dy
        extra = 16 if phase == 0 else 0
        if dx == 1:
            source = low_halo if phase == 0 else cells.at[1, 1, pl.ds(ROW[4], F)]
            target = cells.at[1, y, pl.ds(ROW[0], F + extra)]
        else:
            source = cells.at[1, 1, pl.ds(ROW[1] - extra, F + extra)]
            target = cells.at[1, y, pl.ds(ROW[5] - extra, F + extra)]
        name = ("xy", phase, dx, dy) if dy else ("x", phase, dx)
        return copy(name, source, target, (keeper(share + dx), gy + dy, gz))

    def y_copy(phase, dy, part):
        cells, rows = columns[phase], pl.ds(*PARTS[phase][part])
        return copy(
            ("y", phase, dy, part), cells.at[1, 1, rows], cells.at[1, 1 - dy, rows],
            (gx, gy + dy, gz),
        )

    def z_copy(phase, dz, y, part):
        cells, rows = columns[phase], pl.ds(*PARTS[phase][part])
        return copy(
            ("z", phase, dz, y, part), cells.at[1, y, rows], cells.at[1 - dz, y, rows],
            (gx, gy, gz + dz),
        )

    def zx_copy(phase, dz, y):
        cells, rows = columns[phase], pl.ds(TILE_ABOVE, 160) if phase == 0 else pl.ds(ROW[5], 128)
        return copy(
            ("zx", phase, dz, y), cells.at[1, y, rows], cells.at[1 - dz, y, rows],
            (gx, gy, gz + dz),
        )

    def locate(z, y, inner):
        step = lax.broadcasted_iota(jnp.int32, (4, J), 0)
        if inner:
            rows = column0[z, y, TILE : TILE + 16, :].astype(F32)
            rows = {t + 1: rows[4 * t : 4 * t + 4] for t in range(OWN)}
        else:
            below = column0[z, y, TILE_BELOW : TILE_BELOW + 16, :].astype(F32)
            above = column0[z, y, TILE_ABOVE : TILE_ABOVE + 16, :].astype(F32)
            rows = {0: below[12:16], 5: above[0:4]}
        for l, row in rows.items():
            shift = jnp.where(step == 0, float(l), jnp.where(step == 1, y - 1.0, z - 1.0))
            near[z, y, l, 0:4, :] = row - shift

    begun = set()

    def convolve(phase, cells_of, inner):
        cells = columns[phase]
        scale = [rates[phase, m] * -LOG2E for m in range(2)]
        for b in range(OWN) if inner else (0, 3):
            wanted = range(max(b, 1), min(b + 2, 4) + 1) if inner else (0,) if b == 0 else (5,)
            beside = [(z, y, l) for l in wanted for z, y in cells_of]
            if (phase, b) in begun:
                total = [acc[b, m] for m in range(2)]
            else:
                total = [jnp.zeros((J, F), F32) for m in range(2)]
                begun.add((phase, b))
            for g in range(0, len(beside), 2):
                h, kern = [], [[], []]
                for z, y, l in beside[g : g + 2]:
                    h.append(cells[z, y, ROW[l] : ROW[l] + F, :])
                    dist = None
                    for c in range(3):
                        r = own[b, c] - near[z, y, l, c : c + 1, :]
                        dist = r * r if dist is None else dist + r * r
                    for m in range(2):
                        kern[m].append(jnp.exp2(dist * scale[m]).astype(BF))
                h = jnp.concatenate(h, axis=1)
                for m in range(2):
                    total[m] = total[m] + lax.dot_general(
                        jnp.concatenate(kern[m], axis=1), h, (((1,), (1,)), ((), ())),
                        preferred_element_type=F32,
                    )
            for m in range(2):
                acc[b, m] = total[m]

    def update(phase, bins):
        gathered = [jnp.concatenate([acc[b, m] for b in bins], axis=0).astype(BF) for m in range(2)]
        mixed = None
        for m in range(2):
            term = lax.dot_general(
                conv_w[phase, :, m, :], gathered[m], (((1,), (1,)), ((), ())),
                preferred_element_type=F32,
            )
            mixed = term if mixed is None else mixed + term
        centred = mixed - jnp.mean(mixed, axis=0, keepdims=True)
        spread = jnp.mean(centred * centred, axis=0, keepdims=True)
        normed = (centred * lax.rsqrt(spread + EPSILON)).astype(BF)
        raised = jnp.dot(up_w[phase], normed, preferred_element_type=F32)
        raised = raised + jnp.concatenate([bias_up[phase]] * 2, axis=1)
        hidden = jax.nn.silu(raised).astype(BF)
        change = jnp.dot(down_w[phase], hidden, preferred_element_type=F32)
        change = change + jnp.concatenate([bias_down[phase]] * 2, axis=1)
        for n, b in enumerate(bins):
            before = columns[phase][1, 1, ROW[b + 1] : ROW[b + 1] + F, :].astype(F32)
            live = near[1, 1, b + 1, 3:4, :]
            after = ((before + change[:, J * n : J * (n + 1)]) * live).astype(BF)
            if phase == 0:
                column1[1, 1, ROW[b + 1] : ROW[b + 1] + F, :] = after
            else:
                home[share * OWN + b] = after

    def home_copy(d, part):
        first, count = HOME[part]
        rows = home.at[pl.ds(share * OWN + first, count)]
        return copy(("home", d, part), rows, rows, (share - d, gy, gz))

    def start_z(phase, parts):
        for dz in ENDS:

            @pl.when(has(0, 0, dz))
            def _():
                for part in parts:
                    z_copy(phase, dz, 1, part).start()

    def start_y(phase, parts):
        for dy in ENDS:

            @pl.when(has(0, dy, 0))
            def _():
                for part in parts:
                    y_copy(phase, dy, part).start()

    def start_x(phase):
        for dx in ENDS:
            pl.when(has(dx, 0, 0))(lambda dx=dx: x_copy(phase, dx, 0).start())

    def start_corners(phase):
        for dx, dy in CORNERS:
            pl.when(has(dx, dy, 0))(lambda dx=dx, dy=dy: x_copy(phase, dx, dy).start())

    def start_home(parts):
        for part in parts:
            for d in SHARE_FROM:
                pl.when(share_came(d))(lambda d=d, p=part: home_copy(d, p).start())

    def forward(phase, y, part):
        dy = 1 - y
        pl.when(has(0, -dy, 0))(lambda: y_copy(phase, dy, part).wait_recv())
        for dz in ENDS:
            pl.when(has(0, 0, dz))(lambda dz=dz: z_copy(phase, dz, y, part).start())

    def forward_halo(phase, y):
        dy = 1 - y
        for dx in ENDS:
            pl.when(has(-dx, -dy, 0))(lambda dx=dx: x_copy(phase, dx, dy).wait_recv())
        for dz in ENDS:
            pl.when(has(0, 0, dz))(lambda dz=dz: zx_copy(phase, dz, y).start())

    def receive_z(phase, y, part):
        for dz in ENDS:
            pl.when(has(0, 0, -dz))(lambda dz=dz: z_copy(phase, dz, y, part).wait_recv())

    def receive_zx(phase, y):
        for dz in ENDS:
            pl.when(has(0, 0, -dz))(lambda dz=dz: zx_copy(phase, dz, y).wait_recv())

    def finish_share():
        for d in SHARE_FROM:
            used, device = share_sent(d)
            pl.when(jnp.logical_and(used, device != gx))(lambda d=d: share_copy(d).wait_send())

    def finish_home():
        for d in SHARE_FROM:

            @pl.when(share_came(d))
            def _():
                for part in range(len(HOME)):
                    home_copy(d, part).wait_send()

    def finish(phase):
        parts = range(len(PARTS[phase]))
        for dx in ENDS:
            for dy in (-1, 0, 1):
                pl.when(has(dx, dy, 0))(lambda dx=dx, dy=dy: x_copy(phase, dx, dy).wait_send())
        for dy in ENDS:

            @pl.when(has(0, dy, 0))
            def _():
                for part in parts:
                    y_copy(phase, dy, part).wait_send()

        for dz in ENDS:

            @pl.when(has(0, 0, dz))
            def _():
                for y in range(3):
                    zx_copy(phase, dz, y).wait_send()
                    for part in parts:
                        z_copy(phase, dz, y, part).wait_send()

    def find(phase, cells_of, inner):
        if phase == 0:
            for z, y in cells_of:
                locate(z, y, inner)

    def layer(phase):
        parts = range(len(PARTS[phase]))
        sides, beside = [(0, 1), (2, 1)], [(1, 0), (1, 2)]
        fresh = parts if phase == 0 else parts[1:]
        start_x(phase)
        start_y(phase, fresh)
        start_corners(phase)
        start_z(phase, fresh)
        if phase == 0:
            for b in range(OWN):
                for c in range(3):
                    row = tile[4 * b + c : 4 * b + c + 1, :]
                    row = row - float(b + 1) if c == 0 else row
                    own[b, c] = jnp.broadcast_to(row, (J, J)).T
        find(phase, [(1, 1)], True)
        convolve(phase, [(1, 1)], True)
        if phase == 1:
            finish_share()
            finish(0)
        forward_halo(phase, 1)
        find(phase, [(1, 1)], False)
        convolve(phase, [(1, 1)], False)
        if phase == 1:
            forward(phase, 0, 0)
            forward(phase, 2, 0)
        for part in parts[phase:]:
            forward(phase, 0, part)
            forward(phase, 2, part)
        for part in parts:
            receive_z(phase, 1, part)
        find(phase, sides, True)
        convolve(phase, sides, True)
        find(phase, beside, True)
        convolve(phase, beside, True)
        forward_halo(phase, 0)
        forward_halo(phase, 2)
        receive_zx(phase, 1)
        find(phase, sides, False)
        convolve(phase, sides, False)
        find(phase, beside, False)
        convolve(phase, beside, False)
        for y in (0, 2):
            for part in parts:
                receive_z(phase, y, part)
            find(phase, [(0, y), (2, y)], True)
            convolve(phase, [(0, y), (2, y)], True)
        update(phase, (1, 2))
        if phase == 0:
            start_y(1, (0,))
            start_z(1, (0,))
        else:
            start_home((0,))
        for y in (0, 2):
            receive_zx(phase, y)
            find(phase, [(0, y), (2, y)], False)
            convolve(phase, [(0, y), (2, y)], False)
        update(phase, (0, 3))

    layer(0)
    layer(1)
    start_home((1, 2))
    finish(1)
    finish_home()

    for d in SHARE_FROM:
        used, device = share_sent(d)

        @pl.when(jnp.logical_and(used, device != gx))
        def _():
            for part, (first, count) in enumerate(HOME):
                rows = home.at[pl.ds((gx + d) * OWN + first, count)]
                copy(("home", d, part), rows, rows, (device, gy, gz)).wait_recv()

    held = new_cuts[gx + 1] - new_cuts[gx]
    for slot in range(SLOT_CAP):
        place = jnp.clip(new_cuts[gx] + slot, 0, N_GX * OWN - 1)
        keep = jnp.broadcast_to(held, (F, J)) > slot
        out[slot] = jnp.where(keep, home[place].astype(F32), 0.0).astype(BF)


def local(
    features, positions, counts, old_cuts, new_cuts, radial_rates, conv_weight, up_weight, up_bias,
    down_weight, down_bias,
):
    result = pl.pallas_call(
        kernel,
        out_shape=jax.ShapeDtypeStruct((SLOT_CAP, F, J), BF),
        in_specs=[pl.BlockSpec(memory_space=pl.ANY)] * 11,
        out_specs=pl.BlockSpec(memory_space=pltpu.VMEM),
        scratch_shapes=[
            pltpu.VMEM((SLOT_CAP, F, J), BF),
            pltpu.VMEM((3, SLOT_CAP, J), BF),
            pltpu.SMEM((SLOT_CAP,), jnp.int32),
            pltpu.SMEM((N_GX + 1,), jnp.int32),
            pltpu.SMEM((N_GX + 1,), jnp.int32),
            pltpu.SMEM((2, 2), F32),
            pltpu.VMEM((2, F, 2, F), BF),
            pltpu.VMEM((2, F, HID), BF),
            pltpu.VMEM((2, HID), F32),
            pltpu.VMEM((2, F, HID), BF),
            pltpu.VMEM((2, F), F32),
            pltpu.VMEM((2, HID, F), BF),
            pltpu.VMEM((SLOT_CAP, F, J), BF),
            pltpu.VMEM((SLOT_CAP, 8, J), F32),
            pltpu.VMEM((7, PARCEL, J), BF),
            pltpu.VMEM((7, PARCEL, J), BF),
            pltpu.VMEM((16, J), F32),
            pltpu.VMEM((3, 3, COLUMN, J), BF),
            pltpu.VMEM((3, 3, COLUMN, J), BF),
            pltpu.VMEM((80, J), BF),
            pltpu.VMEM((3, 3, OWN + 2, 8, J), F32),
            pltpu.VMEM((OWN, 3, J, J), F32),
            pltpu.VMEM((OWN, 2, J, F), F32),
            pltpu.VMEM((2, HID, J), F32),
            pltpu.VMEM((2, F, J), F32),
            pltpu.VMEM((N_GX * OWN, F, J), BF),
            pltpu.SemaphoreType.DMA((11,)),
            pltpu.SemaphoreType.DMA((len(NUMBER),)),
            pltpu.SemaphoreType.DMA((len(NUMBER),)),
        ],
        compiler_params=pltpu.CompilerParams(
            collective_id=0, has_side_effects=True, vmem_limit_bytes=60 * 2**20
        ),
    )(
        features.reshape(SLOT_CAP, F, J),
        positions.transpose(1, 2, 3, 0, 4).reshape(3, SLOT_CAP, J),
        counts.reshape(SLOT_CAP),
        old_cuts,
        new_cuts,
        radial_rates,
        conv_weight,
        up_weight.transpose(0, 2, 1),
        up_bias,
        down_weight,
        down_bias,
    )
    return result.reshape(SLOT_CAP, 1, 1, F, J)


def solution(mesh):
    grid = P("gx", "gy", "gz")
    return jax.shard_map(
        local,
        mesh=mesh,
        in_specs=(grid, grid, grid) + (P(),) * 8,
        out_specs=grid,
        check_vma=False,
    )
```

```python
import jax
import jax.numpy as jnp
from jax import lax
from jax.experimental import pallas as pl
from jax.experimental.pallas import tpu as pltpu
from jax.sharding import PartitionSpec as P

MESH = pl.DeviceIdType.MESH
BF = jnp.bfloat16
F32 = jnp.float32
EPSILON = 1e-05
LOG2E = 1.4426950408889634

N_GX, N_GY, N_GZ = 8, 4, 8
SLOT_CAP, OWN = 8, 4
F, J, HID = 64, 128, 256

COLUMN = 432
ROW = (352, 16, 80, 144, 208, 288)
TILE, TILE_ABOVE, TILE_BELOW = 0, 272, 416
PARCEL = 272

SHARE_FROM = {0: (0, 7), 1: (0, 6), -1: (1, 7), 2: (1, 4), -2: (3, 6), 3: (2, 2), -3: (5, 5)}
ENDS = (-1, 1)
CORNERS = ((-1, -1), (1, -1), (-1, 1), (1, 1))
PARTS = (((0, 272),), ((80, 128), (16, 64), (208, 64)))
PART_LAYERS = (((1, 2, 3, 4),), ((2, 3), (1,), (4,)))
INNER, HALO = (1, 2, 3, 4), (0, 5)
HOME = ((1, 2), (0, 1), (3, 1))


def name_copies():
    names = [("share", d) for d in SHARE_FROM]
    for phase in range(2):
        names += [("x", phase, dx) for dx in ENDS]
        names += [("xy", phase, dx, dy) for dx, dy in CORNERS]
        for part in range(len(PARTS[phase])):
            names += [("y", phase, dy, part) for dy in ENDS]
            names += [("z", phase, dz, y, part) for dz in ENDS for y in range(3)]
        names += [("zx", phase, dz, y) for dz in ENDS for y in range(3)]
    names += [("home", d, part) for d in SHARE_FROM for part in range(len(HOME))]
    return {name: number for number, name in enumerate(names)}


NUMBER = name_copies()


def snake(k):
    return k + ((k // 2) % 2) * (1 - 2 * (k % 2))


def gx_partners():
    met = {k: set() for k in range(N_GX)}
    for d, (low, high) in SHARE_FROM.items():
        for k in range(low, high + 1):
            met[k].add(snake(k + d))
            met[snake(k + d)].add(k)
    for s in range(N_GX - 1):
        met[snake(s)].add(snake(s + 1))
        met[snake(s + 1)].add(snake(s))
    return {j: sorted(k for k in met if j in met[k] and j != k) for j in range(N_GX)}


def within(value, low, high):
    return jnp.logical_and(value >= low, value <= high)


def either(conditions):
    result = conditions[0]
    for condition in conditions[1:]:
        result = jnp.logical_or(result, condition)
    return result


def kernel(
    features_in, positions_in, counts_in, old_cuts_in, new_cuts_in, rates_in, conv_w_in, up_w_in,
    up_b_in, down_w_in, down_b_in,
    out,
    features, positions, counts, old_cuts, new_cuts, rates, conv_w, up_w_read, up_b, down_w, down_b,
    up_w, masked, places, parcel, shared, tile, column0, column1, low_halo, near, own, acc, bias_up,
    bias_down, home, load_sem, send_sem, recv_sem,
):
    gx, gy, gz = lax.axis_index("gx"), lax.axis_index("gy"), lax.axis_index("gz")
    share = snake(gx)
    columns = (column0, column1)

    def keeper(s):
        return snake(jnp.clip(s, 0, N_GX - 1))

    def copy(name, source, target, device):
        return pltpu.make_async_remote_copy(
            src_ref=source, dst_ref=target, send_sem=send_sem.at[NUMBER[name]],
            recv_sem=recv_sem.at[NUMBER[name]], device_id=device, device_id_type=MESH,
        )

    def has(dx, dy, dz):
        ok = None
        for place, count, step in ((share, N_GX, dx), (gy, N_GY, dy), (gz, N_GZ, dz)):
            if step:
                here = place < count - 1 if step > 0 else place > 0
                ok = here if ok is None else jnp.logical_and(ok, here)
        return ok

    for cells in columns:

        @pl.when(share == 0)
        def _():
            for y in range(3):
                cells[1, y, ROW[0] : ROW[0] + 80, :] = jnp.zeros((80, J), BF)

        @pl.when(share == N_GX - 1)
        def _():
            for y in range(3):
                cells[1, y, TILE_ABOVE : TILE_ABOVE + 80, :] = jnp.zeros((80, J), BF)

        @pl.when(gy == 0)
        def _():
            cells[1, 0] = jnp.zeros((COLUMN, J), BF)

        @pl.when(gy == N_GY - 1)
        def _():
            cells[1, 2] = jnp.zeros((COLUMN, J), BF)

        @pl.when(gz == 0)
        def _():
            cells[0] = jnp.zeros((3, COLUMN, J), BF)

        @pl.when(gz == N_GZ - 1)
        def _():
            cells[2] = jnp.zeros((3, COLUMN, J), BF)

    partners = []
    for j, near_j in gx_partners().items():
        partners.append(((j, gy, gz), either([gx == k for k in near_j])))
    for dx, dy in CORNERS:
        partners.append(((keeper(share + dx), gy + dy, gz), has(dx, dy, 0)))
    for step in ENDS:
        partners.append(((gx, gy + step, gz), has(0, step, 0)))
        partners.append(((gx, gy, gz + step), has(0, 0, step)))
    barrier = pltpu.get_barrier_semaphore()
    peers = jnp.int32(0)
    for device, there in partners:
        peers = peers + jnp.where(there, 1, 0)

        @pl.when(there)
        def _():
            pl.semaphore_signal(barrier, inc=1, device_id=device, device_id_type=MESH)

    arguments = (
        (counts_in, counts), (old_cuts_in, old_cuts), (features_in, features),
        (positions_in, positions), (up_b_in, up_b), (down_b_in, down_b), (up_w_in, up_w_read),
        (conv_w_in, conv_w), (down_w_in, down_w), (rates_in, rates), (new_cuts_in, new_cuts),
    )
    loads = [
        pltpu.make_async_copy(source, target, load_sem.at[n])
        for n, (source, target) in enumerate(arguments)
    ]
    for load in loads:
        load.start()
    for load in loads[:4]:
        load.wait()

    particle = lax.broadcasted_iota(jnp.int32, (1, J), 1)
    for slot in range(SLOT_CAP):
        live = (particle < counts[slot]).astype(F32)
        masked[slot] = (features[slot].astype(F32) * live).astype(BF)
        for c in range(3):
            places[slot, c : c + 1, :] = positions[c].astype(F32)[slot : slot + 1, :]
        places[slot, 3:4, :] = live

    def share_sent(d):
        low, high = SHARE_FROM[d]
        return within(gx, low, high), keeper(gx + d)

    def share_came(d):
        low, high = SHARE_FROM[d]
        return jnp.logical_and(within(share - d, low, high), share - d != gx)

    def share_copy(d):
        return copy(
            ("share", d), parcel.at[d + 3], shared.at[d + 3], (share_sent(d)[1], gy, gz)
        )

    for d in SHARE_FROM:
        used, device = share_sent(d)

        @pl.when(used)
        def _():
            for t in range(OWN):
                slot = jnp.clip((gx + d) * OWN + t - old_cuts[gx], 0, SLOT_CAP - 1)
                parcel[d + 3, 16 + F * t : 16 + F * (t + 1), :] = masked[slot]
                tile[4 * t : 4 * t + 4, :] = places[slot, 0:4, :]
            parcel[d + 3, 0:16, :] = tile[...].astype(BF)

        @pl.when(jnp.logical_and(used, device == gx))
        def _():
            shared[d + 3] = parcel[d + 3]

    pl.semaphore_wait(barrier, peers)

    for d in SHARE_FROM:
        used, device = share_sent(d)
        pl.when(jnp.logical_and(used, device != gx))(lambda d=d: share_copy(d).start())
    for load in loads[4:]:
        load.wait()
    for phase in range(2):
        for half in range(2):
            row = up_b[phase : phase + 1, J * half : J * (half + 1)]
            bias_up[phase, J * half : J * (half + 1), :] = jnp.broadcast_to(row, (J, J)).T
        row = down_b[phase : phase + 1, :]
        row = jnp.concatenate([row, row], axis=1)
        bias_down[phase] = jnp.broadcast_to(row, (J, J)).T[:F]
        up_w[phase] = up_w_read[phase].astype(F32).T.astype(BF)

    for d in SHARE_FROM:
        pl.when(share_came(d))(lambda d=d: share_copy(d).wait_recv())

    for t in range(OWN):
        place = share * OWN + t
        holder = jnp.int32(0)
        for k in range(1, N_GX):
            holder = holder + jnp.where(old_cuts[k] <= place, 1, 0)
        came = jnp.clip(share - holder + 3, 0, 6)
        column0[1, 1, ROW[t + 1] : ROW[t + 1] + F, :] = shared[came, 16 + F * t : 16 + F * (t + 1), :]
        tile[4 * t : 4 * t + 4, :] = shared[came, 0:16, :].astype(F32)[4 * t : 4 * t + 4]
    column0[1, 1, 0:16, :] = tile[...].astype(BF)
    low_halo[0:F, :] = column0[1, 1, ROW[4] : ROW[4] + F, :]
    low_halo[F : F + 16, :] = tile[...].astype(BF)

    def x_copy(phase, dx, dy):
        cells, y = columns[phase], 1 - dy
        extra = 16 if phase == 0 else 0
        if dx == 1:
            source = low_halo if phase == 0 else cells.at[1, 1, pl.ds(ROW[4], F)]
            target = cells.at[1, y, pl.ds(ROW[0], F + extra)]
        else:
            source = cells.at[1, 1, pl.ds(ROW[1] - extra, F + extra)]
            target = cells.at[1, y, pl.ds(ROW[5] - extra, F + extra)]
        name = ("xy", phase, dx, dy) if dy else ("x", phase, dx)
        return copy(name, source, target, (keeper(share + dx), gy + dy, gz))

    def y_copy(phase, dy, part):
        cells, rows = columns[phase], pl.ds(*PARTS[phase][part])
        return copy(
            ("y", phase, dy, part), cells.at[1, 1, rows], cells.at[1, 1 - dy, rows],
            (gx, gy + dy, gz),
        )

    def z_copy(phase, dz, y, part):
        cells, rows = columns[phase], pl.ds(*PARTS[phase][part])
        return copy(
            ("z", phase, dz, y, part), cells.at[1, y, rows], cells.at[1 - dz, y, rows],
            (gx, gy, gz + dz),
        )

    def zx_copy(phase, dz, y):
        cells, rows = columns[phase], pl.ds(TILE_ABOVE, 160) if phase == 0 else pl.ds(ROW[5], 128)
        return copy(
            ("zx", phase, dz, y), cells.at[1, y, rows], cells.at[1 - dz, y, rows],
            (gx, gy, gz + dz),
        )

    def locate(z, y, inner):
        step = lax.broadcasted_iota(jnp.int32, (4, J), 0)
        if inner:
            rows = column0[z, y, TILE : TILE + 16, :].astype(F32)
            rows = {t + 1: rows[4 * t : 4 * t + 4] for t in range(OWN)}
        else:
            below = column0[z, y, TILE_BELOW : TILE_BELOW + 16, :].astype(F32)
            above = column0[z, y, TILE_ABOVE : TILE_ABOVE + 16, :].astype(F32)
            rows = {0: below[12:16], 5: above[0:4]}
        for l, row in rows.items():
            shift = jnp.where(step == 0, float(l), jnp.where(step == 1, y - 1.0, z - 1.0))
            near[z, y, l, 0:4, :] = row - shift

    begun = set()

    def convolve(phase, cells_of, layers, bins=range(OWN)):
        cells = columns[phase]
        scale = [rates[phase, m] * -LOG2E for m in range(2)]
        for b in bins:
            beside = [(z, y, l) for l in layers if b <= l <= b + 2 for z, y in cells_of]
            if not beside:
                continue
            if (phase, b) in begun:
                total = [acc[b, m] for m in range(2)]
            else:
                total = [jnp.zeros((J, F), F32) for m in range(2)]
                begun.add((phase, b))
            for g in range(0, len(beside), 2):
                h, kern = [], [[], []]
                for z, y, l in beside[g : g + 2]:
                    h.append(cells[z, y, ROW[l] : ROW[l] + F, :])
                    dist = None
                    for c in range(3):
                        r = own[b, c] - near[z, y, l, c : c + 1, :]
                        dist = r * r if dist is None else dist + r * r
                    for m in range(2):
                        kern[m].append(jnp.exp2(dist * scale[m]).astype(BF))
                h = jnp.concatenate(h, axis=1)
                for m in range(2):
                    total[m] = total[m] + lax.dot_general(
                        jnp.concatenate(kern[m], axis=1), h, (((1,), (1,)), ((), ())),
                        preferred_element_type=F32,
                    )
            for m in range(2):
                acc[b, m] = total[m]

    def update(phase, bins):
        gathered = [jnp.concatenate([acc[b, m] for b in bins], axis=0).astype(BF) for m in range(2)]
        mixed = None
        for m in range(2):
            term = lax.dot_general(
                conv_w[phase, :, m, :], gathered[m], (((1,), (1,)), ((), ())),
                preferred_element_type=F32,
            )
            mixed = term if mixed is None else mixed + term
        centred = mixed - jnp.mean(mixed, axis=0, keepdims=True)
        spread = jnp.mean(centred * centred, axis=0, keepdims=True)
        normed = (centred * lax.rsqrt(spread + EPSILON)).astype(BF)
        raised = jnp.dot(up_w[phase], normed, preferred_element_type=F32)
        raised = raised + jnp.concatenate([bias_up[phase]] * 2, axis=1)
        hidden = jax.nn.silu(raised).astype(BF)
        change = jnp.dot(down_w[phase], hidden, preferred_element_type=F32)
        change = change + jnp.concatenate([bias_down[phase]] * 2, axis=1)
        for n, b in enumerate(bins):
            before = columns[phase][1, 1, ROW[b + 1] : ROW[b + 1] + F, :].astype(F32)
            live = near[1, 1, b + 1, 3:4, :]
            after = ((before + change[:, J * n : J * (n + 1)]) * live).astype(BF)
            if phase == 0:
                column1[1, 1, ROW[b + 1] : ROW[b + 1] + F, :] = after
            else:
                home[share * OWN + b] = after

    def home_copy(d, part):
        first, count = HOME[part]
        rows = home.at[pl.ds(share * OWN + first, count)]
        return copy(("home", d, part), rows, rows, (share - d, gy, gz))

    def start_z(phase, parts):
        for dz in ENDS:

            @pl.when(has(0, 0, dz))
            def _():
                for part in parts:
                    z_copy(phase, dz, 1, part).start()

    def start_y(phase, parts):
        for dy in ENDS:

            @pl.when(has(0, dy, 0))
            def _():
                for part in parts:
                    y_copy(phase, dy, part).start()

    def start_x(phase):
        for dx in ENDS:
            pl.when(has(dx, 0, 0))(lambda dx=dx: x_copy(phase, dx, 0).start())

    def start_corners(phase):
        for dx, dy in CORNERS:
            pl.when(has(dx, dy, 0))(lambda dx=dx, dy=dy: x_copy(phase, dx, dy).start())

    def start_home(parts):
        for part in parts:
            for d in SHARE_FROM:
                pl.when(share_came(d))(lambda d=d, p=part: home_copy(d, p).start())

    def forward(phase, y, part):
        dy = 1 - y
        pl.when(has(0, -dy, 0))(lambda: y_copy(phase, dy, part).wait_recv())
        for dz in ENDS:
            pl.when(has(0, 0, dz))(lambda dz=dz: z_copy(phase, dz, y, part).start())

    def forward_halo(phase, y):
        dy = 1 - y
        for dx in ENDS:
            pl.when(has(-dx, -dy, 0))(lambda dx=dx: x_copy(phase, dx, dy).wait_recv())
        for dz in ENDS:
            pl.when(has(0, 0, dz))(lambda dz=dz: zx_copy(phase, dz, y).start())

    def receive_z(phase, y, part):
        for dz in ENDS:
            pl.when(has(0, 0, -dz))(lambda dz=dz: z_copy(phase, dz, y, part).wait_recv())

    def receive_zx(phase, y):
        for dz in ENDS:
            pl.when(has(0, 0, -dz))(lambda dz=dz: zx_copy(phase, dz, y).wait_recv())

    def finish_share():
        for d in SHARE_FROM:
            used, device = share_sent(d)
            pl.when(jnp.logical_and(used, device != gx))(lambda d=d: share_copy(d).wait_send())

    def finish_home():
        for d in SHARE_FROM:

            @pl.when(share_came(d))
            def _():
                for part in range(len(HOME)):
                    home_copy(d, part).wait_send()

    def finish(phase):
        parts = range(len(PARTS[phase]))
        for dx in ENDS:
            for dy in (-1, 0, 1):
                pl.when(has(dx, dy, 0))(lambda dx=dx, dy=dy: x_copy(phase, dx, dy).wait_send())
        for dy in ENDS:

            @pl.when(has(0, dy, 0))
            def _():
                for part in parts:
                    y_copy(phase, dy, part).wait_send()

        for dz in ENDS:

            @pl.when(has(0, 0, dz))
            def _():
                for y in range(3):
                    zx_copy(phase, dz, y).wait_send()
                    for part in parts:
                        z_copy(phase, dz, y, part).wait_send()

    def find(phase, cells_of, inner):
        if phase == 0:
            for z, y in cells_of:
                locate(z, y, inner)

    def layer(phase):
        parts = range(len(PARTS[phase]))
        sides, beside = [(0, 1), (2, 1)], [(1, 0), (1, 2)]
        fresh = parts if phase == 0 else parts[1:]
        start_x(phase)
        start_y(phase, fresh)
        start_corners(phase)
        start_z(phase, fresh)
        if phase == 0:
            for b in range(OWN):
                for c in range(3):
                    row = tile[4 * b + c : 4 * b + c + 1, :]
                    row = row - float(b + 1) if c == 0 else row
                    own[b, c] = jnp.broadcast_to(row, (J, J)).T
        find(phase, [(1, 1)], True)
        convolve(phase, [(1, 1)], INNER)
        if phase == 1:
            finish_share()
            finish(0)
            forward(phase, 0, 0)
            forward(phase, 2, 0)
        forward_halo(phase, 1)
        find(phase, [(1, 1)], False)
        convolve(phase, [(1, 1)], HALO)
        corners = [[(0, 0), (2, 0)], [(0, 2), (2, 2)]]
        if phase == 0:
            for part in parts:
                forward(phase, 0, part)
                forward(phase, 2, part)
            for part in parts:
                receive_z(phase, 1, part)
                if part == 0:
                    find(phase, sides, True)
                convolve(phase, sides, PART_LAYERS[phase][part])
            find(phase, beside, True)
            convolve(phase, beside, INNER)
            forward_halo(phase, 0)
            forward_halo(phase, 2)
        else:
            receive_z(phase, 1, 0)
            convolve(phase, sides, PART_LAYERS[phase][0])
            convolve(phase, beside, PART_LAYERS[phase][0])
            for part in parts[1:]:
                forward(phase, 0, part)
                forward(phase, 2, part)
            for part in parts[1:]:
                receive_z(phase, 1, part)
            convolve(phase, sides, (1, 4))
            convolve(phase, beside, (1, 4))
            forward_halo(phase, 0)
            forward_halo(phase, 2)
        for y in (0, 2):
            receive_z(phase, y, 0)
            find(phase, corners[y // 2], True)
            convolve(phase, corners[y // 2], PART_LAYERS[phase][0])
        receive_zx(phase, 1)
        find(phase, sides, False)
        convolve(phase, sides, HALO)
        find(phase, beside, False)
        convolve(phase, beside, HALO)
        rest = [l for part in parts[1:] for l in PART_LAYERS[phase][part]]
        for y in (0, 2):
            for part in parts[1:]:
                receive_z(phase, y, part)
            convolve(phase, corners[y // 2], rest, (1, 2))
        update(phase, (1, 2))
        if phase == 0:
            start_y(1, (0,))
            start_z(1, (0,))
        else:
            start_home((0,))
        for y in (0, 2):
            convolve(phase, corners[y // 2], rest, (0, 3))
        for y in (0, 2):
            receive_zx(phase, y)
            find(phase, corners[y // 2], False)
            convolve(phase, corners[y // 2], HALO)
        update(phase, (0, 3))

    layer(0)
    layer(1)
    start_home((1, 2))
    finish(1)
    finish_home()

    for d in SHARE_FROM:
        used, device = share_sent(d)

        @pl.when(jnp.logical_and(used, device != gx))
        def _():
            for part, (first, count) in enumerate(HOME):
                rows = home.at[pl.ds((gx + d) * OWN + first, count)]
                copy(("home", d, part), rows, rows, (device, gy, gz)).wait_recv()

    held = new_cuts[gx + 1] - new_cuts[gx]
    for slot in range(SLOT_CAP):
        place = jnp.clip(new_cuts[gx] + slot, 0, N_GX * OWN - 1)
        keep = jnp.broadcast_to(held, (F, J)) > slot
        out[slot] = jnp.where(keep, home[place].astype(F32), 0.0).astype(BF)


def local(
    features, positions, counts, old_cuts, new_cuts, radial_rates, conv_weight, up_weight, up_bias,
    down_weight, down_bias,
):
    result = pl.pallas_call(
        kernel,
        out_shape=pltpu.VMEM((SLOT_CAP, F, J), BF),
        in_specs=[pl.BlockSpec(memory_space=pl.ANY)] * 11,
        out_specs=pl.BlockSpec(memory_space=pltpu.VMEM),
        scratch_shapes=[
            pltpu.VMEM((SLOT_CAP, F, J), BF),
            pltpu.VMEM((3, SLOT_CAP, J), BF),
            pltpu.SMEM((SLOT_CAP,), jnp.int32),
            pltpu.SMEM((N_GX + 1,), jnp.int32),
            pltpu.SMEM((N_GX + 1,), jnp.int32),
            pltpu.SMEM((2, 2), F32),
            pltpu.VMEM((2, F, 2, F), BF),
            pltpu.VMEM((2, F, HID), BF),
            pltpu.VMEM((2, HID), F32),
            pltpu.VMEM((2, F, HID), BF),
            pltpu.VMEM((2, F), F32),
            pltpu.VMEM((2, HID, F), BF),
            pltpu.VMEM((SLOT_CAP, F, J), BF),
            pltpu.VMEM((SLOT_CAP, 8, J), F32),
            pltpu.VMEM((7, PARCEL, J), BF),
            pltpu.VMEM((7, PARCEL, J), BF),
            pltpu.VMEM((16, J), F32),
            pltpu.VMEM((3, 3, COLUMN, J), BF),
            pltpu.VMEM((3, 3, COLUMN, J), BF),
            pltpu.VMEM((80, J), BF),
            pltpu.VMEM((3, 3, OWN + 2, 8, J), F32),
            pltpu.VMEM((OWN, 3, J, J), F32),
            pltpu.VMEM((OWN, 2, J, F), F32),
            pltpu.VMEM((2, HID, J), F32),
            pltpu.VMEM((2, F, J), F32),
            pltpu.VMEM((N_GX * OWN, F, J), BF),
            pltpu.SemaphoreType.DMA((11,)),
            pltpu.SemaphoreType.DMA((len(NUMBER),)),
            pltpu.SemaphoreType.DMA((len(NUMBER),)),
        ],
        compiler_params=pltpu.CompilerParams(
            collective_id=0, has_side_effects=True, vmem_limit_bytes=60 * 2**20
        ),
    )(
        features.reshape(SLOT_CAP, F, J),
        positions.transpose(1, 2, 3, 0, 4).reshape(3, SLOT_CAP, J),
        counts.reshape(SLOT_CAP),
        old_cuts,
        new_cuts,
        radial_rates,
        conv_weight,
        up_weight.transpose(0, 2, 1),
        up_bias,
        down_weight,
        down_bias,
    )
    return result.reshape(SLOT_CAP, 1, 1, F, J)


def solution(mesh):
    grid = P("gx", "gy", "gz")
    return jax.shard_map(
        local,
        mesh=mesh,
        in_specs=(grid, grid, grid) + (P(),) * 8,
        out_specs=grid,
        check_vma=False,
    )
```

```python
import jax
import jax.numpy as jnp
from jax import lax
from jax.experimental import pallas as pl
from jax.experimental.pallas import tpu as pltpu
from jax.sharding import PartitionSpec as P

MESH = pl.DeviceIdType.MESH
BF = jnp.bfloat16
F32 = jnp.float32
EPSILON = 1e-05
LOG2E = 1.4426950408889634

N_GX, N_GY, N_GZ = 8, 4, 8
SLOT_CAP, OWN = 8, 4
F, J, HID = 64, 128, 256

COLUMN = 432
ROW = (352, 16, 80, 144, 208, 288)
TILE, TILE_ABOVE, TILE_BELOW = 0, 272, 416
PARCEL = 272

SHARE_FROM = {0: (0, 7), 1: (0, 6), -1: (1, 7), 2: (1, 4), -2: (3, 6), 3: (2, 2), -3: (5, 5)}
ENDS = (-1, 1)
CORNERS = ((-1, -1), (1, -1), (-1, 1), (1, 1))
PARTS = (((0, 272),), ((80, 128), (16, 64), (208, 64)))
PART_LAYERS = (((1, 2, 3, 4),), ((2, 3), (1,), (4,)))
INNER, HALO = (1, 2, 3, 4), (0, 5)
HOME = ((1, 2), (0, 1), (3, 1))


def name_copies():
    names = [("share", d) for d in SHARE_FROM]
    for phase in range(2):
        names += [("x", phase, dx) for dx in ENDS]
        names += [("xy", phase, dx, dy) for dx, dy in CORNERS]
        for part in range(len(PARTS[phase])):
            names += [("y", phase, dy, part) for dy in ENDS]
            names += [("z", phase, dz, y, part) for dz in ENDS for y in range(3)]
        names += [("zx", phase, dz, y) for dz in ENDS for y in range(3)]
    names += [("home", d, part) for d in SHARE_FROM for part in range(len(HOME))]
    return {name: number for number, name in enumerate(names)}


NUMBER = name_copies()


def snake(k):
    return k + ((k // 2) % 2) * (1 - 2 * (k % 2))


def gx_partners():
    met = {k: set() for k in range(N_GX)}
    for d, (low, high) in SHARE_FROM.items():
        for k in range(low, high + 1):
            met[k].add(snake(k + d))
            met[snake(k + d)].add(k)
    for s in range(N_GX - 1):
        met[snake(s)].add(snake(s + 1))
        met[snake(s + 1)].add(snake(s))
    return {j: sorted(k for k in met if j in met[k] and j != k) for j in range(N_GX)}


def within(value, low, high):
    return jnp.logical_and(value >= low, value <= high)


def either(conditions):
    result = conditions[0]
    for condition in conditions[1:]:
        result = jnp.logical_or(result, condition)
    return result


def kernel(
    features_in, positions_in, counts_in, old_cuts_in, new_cuts_in, rates_in, conv_w_in, up_w_in,
    up_b_in, down_w_in, down_b_in,
    out,
    features, positions, counts, old_cuts, new_cuts, rates, conv_w, up_w_read, up_b, down_w, down_b,
    up_w, masked, places, parcel, shared, tile, column0, column1, low_halo, near, own, acc, bias_up,
    bias_down, home, load_sem, send_sem, recv_sem,
):
    gx, gy, gz = lax.axis_index("gx"), lax.axis_index("gy"), lax.axis_index("gz")
    share = snake(gx)
    columns = (column0, column1)

    def keeper(s):
        return snake(jnp.clip(s, 0, N_GX - 1))

    def copy(name, source, target, device):
        return pltpu.make_async_remote_copy(
            src_ref=source, dst_ref=target, send_sem=send_sem.at[NUMBER[name]],
            recv_sem=recv_sem.at[NUMBER[name]], device_id=device, device_id_type=MESH,
        )

    def has(dx, dy, dz):
        ok = None
        for place, count, step in ((share, N_GX, dx), (gy, N_GY, dy), (gz, N_GZ, dz)):
            if step:
                here = place < count - 1 if step > 0 else place > 0
                ok = here if ok is None else jnp.logical_and(ok, here)
        return ok

    for cells in columns:

        @pl.when(share == 0)
        def _():
            for y in range(3):
                cells[1, y, ROW[0] : ROW[0] + 80, :] = jnp.zeros((80, J), BF)

        @pl.when(share == N_GX - 1)
        def _():
            for y in range(3):
                cells[1, y, TILE_ABOVE : TILE_ABOVE + 80, :] = jnp.zeros((80, J), BF)

        @pl.when(gy == 0)
        def _():
            cells[1, 0] = jnp.zeros((COLUMN, J), BF)

        @pl.when(gy == N_GY - 1)
        def _():
            cells[1, 2] = jnp.zeros((COLUMN, J), BF)

        @pl.when(gz == 0)
        def _():
            cells[0] = jnp.zeros((3, COLUMN, J), BF)

        @pl.when(gz == N_GZ - 1)
        def _():
            cells[2] = jnp.zeros((3, COLUMN, J), BF)

    partners = []
    for j, near_j in gx_partners().items():
        partners.append(((j, gy, gz), either([gx == k for k in near_j])))
    for dx, dy in CORNERS:
        partners.append(((keeper(share + dx), gy + dy, gz), has(dx, dy, 0)))
    for step in ENDS:
        partners.append(((gx, gy + step, gz), has(0, step, 0)))
        partners.append(((gx, gy, gz + step), has(0, 0, step)))
    barrier = pltpu.get_barrier_semaphore()
    peers = jnp.int32(0)
    for device, there in partners:
        peers = peers + jnp.where(there, 1, 0)

        @pl.when(there)
        def _():
            pl.semaphore_signal(barrier, inc=1, device_id=device, device_id_type=MESH)

    arguments = (
        (counts_in, counts), (old_cuts_in, old_cuts), (features_in, features),
        (positions_in, positions), (up_b_in, up_b), (down_b_in, down_b), (up_w_in, up_w_read),
        (conv_w_in, conv_w), (down_w_in, down_w), (rates_in, rates), (new_cuts_in, new_cuts),
    )
    loads = [
        pltpu.make_async_copy(source, target, load_sem.at[n])
        for n, (source, target) in enumerate(arguments)
    ]
    for load in loads:
        load.start()
    for load in loads[:4]:
        load.wait()

    particle = lax.broadcasted_iota(jnp.int32, (1, J), 1)
    for slot in range(SLOT_CAP):
        live = (particle < counts[slot]).astype(F32)
        masked[slot] = (features[slot].astype(F32) * live).astype(BF)
        for c in range(3):
            places[slot, c : c + 1, :] = positions[c].astype(F32)[slot : slot + 1, :]
        places[slot, 3:4, :] = live

    def share_sent(d):
        low, high = SHARE_FROM[d]
        return within(gx, low, high), keeper(gx + d)

    def share_came(d):
        low, high = SHARE_FROM[d]
        return jnp.logical_and(within(share - d, low, high), share - d != gx)

    def share_copy(d):
        return copy(
            ("share", d), parcel.at[d + 3], shared.at[d + 3], (share_sent(d)[1], gy, gz)
        )

    for d in SHARE_FROM:
        used, device = share_sent(d)

        @pl.when(used)
        def _():
            for t in range(OWN):
                slot = jnp.clip((gx + d) * OWN + t - old_cuts[gx], 0, SLOT_CAP - 1)
                parcel[d + 3, 16 + F * t : 16 + F * (t + 1), :] = masked[slot]
                tile[4 * t : 4 * t + 4, :] = places[slot, 0:4, :]
            parcel[d + 3, 0:16, :] = tile[...].astype(BF)

        @pl.when(jnp.logical_and(used, device == gx))
        def _():
            shared[d + 3] = parcel[d + 3]

    pl.semaphore_wait(barrier, peers)

    for d in SHARE_FROM:
        used, device = share_sent(d)
        pl.when(jnp.logical_and(used, device != gx))(lambda d=d: share_copy(d).start())
    for load in loads[4:]:
        load.wait()
    for phase in range(2):
        for half in range(2):
            row = up_b[phase : phase + 1, J * half : J * (half + 1)]
            bias_up[phase, J * half : J * (half + 1), :] = jnp.broadcast_to(row, (J, J)).T
        row = down_b[phase : phase + 1, :]
        row = jnp.concatenate([row, row], axis=1)
        bias_down[phase] = jnp.broadcast_to(row, (J, J)).T[:F]
        up_w[phase] = up_w_read[phase].astype(F32).T.astype(BF)

    for d in SHARE_FROM:
        pl.when(share_came(d))(lambda d=d: share_copy(d).wait_recv())

    for t in range(OWN):
        place = share * OWN + t
        holder = jnp.int32(0)
        for k in range(1, N_GX):
            holder = holder + jnp.where(old_cuts[k] <= place, 1, 0)
        came = jnp.clip(share - holder + 3, 0, 6)
        column0[1, 1, ROW[t + 1] : ROW[t + 1] + F, :] = shared[came, 16 + F * t : 16 + F * (t + 1), :]
        tile[4 * t : 4 * t + 4, :] = shared[came, 0:16, :].astype(F32)[4 * t : 4 * t + 4]
    column0[1, 1, 0:16, :] = tile[...].astype(BF)
    low_halo[0:F, :] = column0[1, 1, ROW[4] : ROW[4] + F, :]
    low_halo[F : F + 16, :] = tile[...].astype(BF)

    def x_copy(phase, dx, dy):
        cells, y = columns[phase], 1 - dy
        extra = 16 if phase == 0 else 0
        if dx == 1:
            source = low_halo if phase == 0 else cells.at[1, 1, pl.ds(ROW[4], F)]
            target = cells.at[1, y, pl.ds(ROW[0], F + extra)]
        else:
            source = cells.at[1, 1, pl.ds(ROW[1] - extra, F + extra)]
            target = cells.at[1, y, pl.ds(ROW[5] - extra, F + extra)]
        name = ("xy", phase, dx, dy) if dy else ("x", phase, dx)
        return copy(name, source, target, (keeper(share + dx), gy + dy, gz))

    def y_copy(phase, dy, part):
        cells, rows = columns[phase], pl.ds(*PARTS[phase][part])
        return copy(
            ("y", phase, dy, part), cells.at[1, 1, rows], cells.at[1, 1 - dy, rows],
            (gx, gy + dy, gz),
        )

    def z_copy(phase, dz, y, part):
        cells, rows = columns[phase], pl.ds(*PARTS[phase][part])
        return copy(
            ("z", phase, dz, y, part), cells.at[1, y, rows], cells.at[1 - dz, y, rows],
            (gx, gy, gz + dz),
        )

    def zx_copy(phase, dz, y):
        cells, rows = columns[phase], pl.ds(TILE_ABOVE, 160) if phase == 0 else pl.ds(ROW[5], 128)
        return copy(
            ("zx", phase, dz, y), cells.at[1, y, rows], cells.at[1 - dz, y, rows],
            (gx, gy, gz + dz),
        )

    def locate(z, y, inner):
        step = lax.broadcasted_iota(jnp.int32, (4, J), 0)
        if inner:
            rows = column0[z, y, TILE : TILE + 16, :].astype(F32)
            rows = {t + 1: rows[4 * t : 4 * t + 4] for t in range(OWN)}
        else:
            below = column0[z, y, TILE_BELOW : TILE_BELOW + 16, :].astype(F32)
            above = column0[z, y, TILE_ABOVE : TILE_ABOVE + 16, :].astype(F32)
            rows = {0: below[12:16], 5: above[0:4]}
        for l, row in rows.items():
            shift = jnp.where(step == 0, float(l), jnp.where(step == 1, y - 1.0, z - 1.0))
            near[z, y, l, 0:4, :] = row - shift

    begun = set()

    def convolve(phase, cells_of, layers, bins=range(OWN)):
        cells = columns[phase]
        scale = [rates[phase, m] * -LOG2E for m in range(2)]
        for b in bins:
            beside = [(z, y, l) for l in layers if b <= l <= b + 2 for z, y in cells_of]
            if not beside:
                continue
            if (phase, b) in begun:
                total = [acc[b, m] for m in range(2)]
            else:
                total = [jnp.zeros((J, F), F32) for m in range(2)]
                begun.add((phase, b))
            for g in range(0, len(beside), 2):
                h, kern = [], [[], []]
                for z, y, l in beside[g : g + 2]:
                    h.append(cells[z, y, ROW[l] : ROW[l] + F, :])
                    dist = None
                    for c in range(3):
                        r = own[b, c] - near[z, y, l, c : c + 1, :]
                        dist = r * r if dist is None else dist + r * r
                    for m in range(2):
                        kern[m].append(jnp.exp2(dist * scale[m]).astype(BF))
                h = jnp.concatenate(h, axis=1)
                for m in range(2):
                    total[m] = total[m] + lax.dot_general(
                        jnp.concatenate(kern[m], axis=1), h, (((1,), (1,)), ((), ())),
                        preferred_element_type=F32,
                    )
            for m in range(2):
                acc[b, m] = total[m]

    def update(phase, bins):
        gathered = [jnp.concatenate([acc[b, m] for b in bins], axis=0).astype(BF) for m in range(2)]
        mixed = None
        for m in range(2):
            term = lax.dot_general(
                conv_w[phase, :, m, :], gathered[m], (((1,), (1,)), ((), ())),
                preferred_element_type=F32,
            )
            mixed = term if mixed is None else mixed + term
        centred = mixed - jnp.mean(mixed, axis=0, keepdims=True)
        spread = jnp.mean(centred * centred, axis=0, keepdims=True)
        normed = (centred * lax.rsqrt(spread + EPSILON)).astype(BF)
        raised = jnp.dot(up_w[phase], normed, preferred_element_type=F32)
        raised = raised + jnp.concatenate([bias_up[phase]] * 2, axis=1)
        hidden = jax.nn.silu(raised).astype(BF)
        change = jnp.dot(down_w[phase], hidden, preferred_element_type=F32)
        change = change + jnp.concatenate([bias_down[phase]] * 2, axis=1)
        for n, b in enumerate(bins):
            before = columns[phase][1, 1, ROW[b + 1] : ROW[b + 1] + F, :].astype(F32)
            live = near[1, 1, b + 1, 3:4, :]
            after = ((before + change[:, J * n : J * (n + 1)]) * live).astype(BF)
            if phase == 0:
                column1[1, 1, ROW[b + 1] : ROW[b + 1] + F, :] = after
            else:
                home[share * OWN + b] = after

    def home_copy(d, part):
        first, count = HOME[part]
        rows = home.at[pl.ds(share * OWN + first, count)]
        return copy(("home", d, part), rows, rows, (share - d, gy, gz))

    def start_z(phase, parts):
        for dz in ENDS:

            @pl.when(has(0, 0, dz))
            def _():
                for part in parts:
                    z_copy(phase, dz, 1, part).start()

    def start_y(phase, parts):
        for dy in ENDS:

            @pl.when(has(0, dy, 0))
            def _():
                for part in parts:
                    y_copy(phase, dy, part).start()

    def start_x(phase):
        for dx in ENDS:
            pl.when(has(dx, 0, 0))(lambda dx=dx: x_copy(phase, dx, 0).start())

    def start_corners(phase):
        for dx, dy in CORNERS:
            pl.when(has(dx, dy, 0))(lambda dx=dx, dy=dy: x_copy(phase, dx, dy).start())

    def start_home(parts):
        for part in parts:
            for d in SHARE_FROM:
                pl.when(share_came(d))(lambda d=d, p=part: home_copy(d, p).start())

    def forward(phase, y, part):
        dy = 1 - y
        pl.when(has(0, -dy, 0))(lambda: y_copy(phase, dy, part).wait_recv())
        for dz in ENDS:
            pl.when(has(0, 0, dz))(lambda dz=dz: z_copy(phase, dz, y, part).start())

    def forward_halo(phase, y):
        dy = 1 - y
        for dx in ENDS:
            pl.when(has(-dx, -dy, 0))(lambda dx=dx: x_copy(phase, dx, dy).wait_recv())
        for dz in ENDS:
            pl.when(has(0, 0, dz))(lambda dz=dz: zx_copy(phase, dz, y).start())

    def receive_z(phase, y, part):
        for dz in ENDS:
            pl.when(has(0, 0, -dz))(lambda dz=dz: z_copy(phase, dz, y, part).wait_recv())

    def receive_zx(phase, y):
        for dz in ENDS:
            pl.when(has(0, 0, -dz))(lambda dz=dz: zx_copy(phase, dz, y).wait_recv())

    def finish_share():
        for d in SHARE_FROM:
            used, device = share_sent(d)
            pl.when(jnp.logical_and(used, device != gx))(lambda d=d: share_copy(d).wait_send())

    def finish_home():
        for d in SHARE_FROM:

            @pl.when(share_came(d))
            def _():
                for part in range(len(HOME)):
                    home_copy(d, part).wait_send()

    def finish(phase):
        parts = range(len(PARTS[phase]))
        for dx in ENDS:
            for dy in (-1, 0, 1):
                pl.when(has(dx, dy, 0))(lambda dx=dx, dy=dy: x_copy(phase, dx, dy).wait_send())
        for dy in ENDS:

            @pl.when(has(0, dy, 0))
            def _():
                for part in parts:
                    y_copy(phase, dy, part).wait_send()

        for dz in ENDS:

            @pl.when(has(0, 0, dz))
            def _():
                for y in range(3):
                    zx_copy(phase, dz, y).wait_send()
                    for part in parts:
                        z_copy(phase, dz, y, part).wait_send()

    def find(phase, cells_of, inner):
        if phase == 0:
            for z, y in cells_of:
                locate(z, y, inner)

    def layer(phase):
        parts = range(len(PARTS[phase]))
        sides, beside = [(0, 1), (2, 1)], [(1, 0), (1, 2)]
        fresh = parts if phase == 0 else parts[1:]
        start_x(phase)
        start_y(phase, fresh)
        start_corners(phase)
        start_z(phase, fresh)
        if phase == 0:
            for b in range(OWN):
                for c in range(3):
                    row = tile[4 * b + c : 4 * b + c + 1, :]
                    row = row - float(b + 1) if c == 0 else row
                    own[b, c] = jnp.broadcast_to(row, (J, J)).T
        find(phase, [(1, 1)], True)
        convolve(phase, [(1, 1)], INNER)
        if phase == 1:
            forward(phase, 0, 0)
            forward(phase, 2, 0)
        forward_halo(phase, 1)
        find(phase, [(1, 1)], False)
        convolve(phase, [(1, 1)], HALO)
        corners = [[(0, 0), (2, 0)], [(0, 2), (2, 2)]]
        if phase == 0:
            for part in parts:
                forward(phase, 0, part)
                forward(phase, 2, part)
            for part in parts:
                receive_z(phase, 1, part)
                if part == 0:
                    find(phase, sides, True)
                convolve(phase, sides, PART_LAYERS[phase][part])
            find(phase, beside, True)
            convolve(phase, beside, INNER)
            forward_halo(phase, 0)
            forward_halo(phase, 2)
        else:
            receive_z(phase, 1, 0)
            convolve(phase, sides, PART_LAYERS[phase][0])
            convolve(phase, beside, PART_LAYERS[phase][0])
            for part in parts[1:]:
                forward(phase, 0, part)
                forward(phase, 2, part)
            for part in parts[1:]:
                receive_z(phase, 1, part)
            convolve(phase, sides, (1, 4))
            convolve(phase, beside, (1, 4))
            forward_halo(phase, 0)
            forward_halo(phase, 2)
        for y in (0, 2):
            receive_z(phase, y, 0)
            find(phase, corners[y // 2], True)
            convolve(phase, corners[y // 2], PART_LAYERS[phase][0])
        receive_zx(phase, 1)
        find(phase, sides, False)
        convolve(phase, sides, HALO)
        find(phase, beside, False)
        convolve(phase, beside, HALO)
        rest = [l for part in parts[1:] for l in PART_LAYERS[phase][part]]
        for y in (0, 2):
            for part in parts[1:]:
                receive_z(phase, y, part)
            convolve(phase, corners[y // 2], rest, (1, 2))
        update(phase, (1, 2))
        if phase == 0:
            start_y(1, (0,))
            start_z(1, (0,))
        else:
            start_home((0,))
        for y in (0, 2):
            convolve(phase, corners[y // 2], rest, (0, 3))
        for y in (0, 2):
            receive_zx(phase, y)
            find(phase, corners[y // 2], False)
            convolve(phase, corners[y // 2], HALO)
        update(phase, (0, 3))

    layer(0)
    layer(1)
    start_home((1, 2))
    finish_share()
    finish(0)
    finish(1)
    finish_home()

    for d in SHARE_FROM:
        used, device = share_sent(d)

        @pl.when(jnp.logical_and(used, device != gx))
        def _():
            for part, (first, count) in enumerate(HOME):
                rows = home.at[pl.ds((gx + d) * OWN + first, count)]
                copy(("home", d, part), rows, rows, (device, gy, gz)).wait_recv()

    held = new_cuts[gx + 1] - new_cuts[gx]
    for slot in range(SLOT_CAP):
        place = jnp.clip(new_cuts[gx] + slot, 0, N_GX * OWN - 1)
        keep = jnp.broadcast_to(held, (F, J)) > slot
        out[slot] = jnp.where(keep, home[place].astype(F32), 0.0).astype(BF)


def local(
    features, positions, counts, old_cuts, new_cuts, radial_rates, conv_weight, up_weight, up_bias,
    down_weight, down_bias,
):
    result = pl.pallas_call(
        kernel,
        out_shape=pltpu.VMEM((SLOT_CAP, F, J), BF),
        in_specs=[pl.BlockSpec(memory_space=pl.ANY)] * 11,
        out_specs=pl.BlockSpec(memory_space=pltpu.VMEM),
        scratch_shapes=[
            pltpu.VMEM((SLOT_CAP, F, J), BF),
            pltpu.VMEM((3, SLOT_CAP, J), BF),
            pltpu.SMEM((SLOT_CAP,), jnp.int32),
            pltpu.SMEM((N_GX + 1,), jnp.int32),
            pltpu.SMEM((N_GX + 1,), jnp.int32),
            pltpu.SMEM((2, 2), F32),
            pltpu.VMEM((2, F, 2, F), BF),
            pltpu.VMEM((2, F, HID), BF),
            pltpu.VMEM((2, HID), F32),
            pltpu.VMEM((2, F, HID), BF),
            pltpu.VMEM((2, F), F32),
            pltpu.VMEM((2, HID, F), BF),
            pltpu.VMEM((SLOT_CAP, F, J), BF),
            pltpu.VMEM((SLOT_CAP, 8, J), F32),
            pltpu.VMEM((7, PARCEL, J), BF),
            pltpu.VMEM((7, PARCEL, J), BF),
            pltpu.VMEM((16, J), F32),
            pltpu.VMEM((3, 3, COLUMN, J), BF),
            pltpu.VMEM((3, 3, COLUMN, J), BF),
            pltpu.VMEM((80, J), BF),
            pltpu.VMEM((3, 3, OWN + 2, 8, J), F32),
            pltpu.VMEM((OWN, 3, J, J), F32),
            pltpu.VMEM((OWN, 2, J, F), F32),
            pltpu.VMEM((2, HID, J), F32),
            pltpu.VMEM((2, F, J), F32),
            pltpu.VMEM((N_GX * OWN, F, J), BF),
            pltpu.SemaphoreType.DMA((11,)),
            pltpu.SemaphoreType.DMA((len(NUMBER),)),
            pltpu.SemaphoreType.DMA((len(NUMBER),)),
        ],
        compiler_params=pltpu.CompilerParams(
            collective_id=0, has_side_effects=True, vmem_limit_bytes=60 * 2**20
        ),
    )(
        features.reshape(SLOT_CAP, F, J),
        positions.transpose(1, 2, 3, 0, 4).reshape(3, SLOT_CAP, J),
        counts.reshape(SLOT_CAP),
        old_cuts,
        new_cuts,
        radial_rates,
        conv_weight,
        up_weight.transpose(0, 2, 1),
        up_bias,
        down_weight,
        down_bias,
    )
    return result.reshape(SLOT_CAP, 1, 1, F, J)


def solution(mesh):
    grid = P("gx", "gy", "gz")
    return jax.shard_map(
        local,
        mesh=mesh,
        in_specs=(grid, grid, grid) + (P(),) * 8,
        out_specs=grid,
        check_vma=False,
    )
```
